32 devices in a mesh: chan: 4 (over z), rad: 8 (over y, x, core).
Axes of the slice: x: 2, y: 2, z: 4, core: 2. Of those that a mesh axis runs over, the one named last changes fastest.
Arguments:
- vectors: float32 [1, 2, 104, 512, 512], P(None, None, 'chan', 'rad'), may hold values from -6 to 6
- eigenvectors: float32 [2, 512, 512], replicated, may hold values from -0.1875 to 0.1875
- energies: float32 [512], replicated, may hold values from 0 to 2
- widths: float32 [512], replicated, may hold values from 0 to 1
- shift_energy: float32 [1], replicated, may hold values from 0.5 to 2
- shift_width: float32 [1], replicated, may hold values from 0.5 to 1
- slot_channel: int32 [104], replicated, may hold values from 0 to 103, as said below
- partners: int32 [104, 12], replicated, may hold values from 0 to 103
- multipole: int32 [104, 12], replicated, may hold values from 0 to 3
- counts: int32 [104], replicated, may hold values from 1 to 12, as said below
- angular: float32 [104, 12], replicated, may hold values from -12 to 12
Outputs:
- update: float32 [1, 2, 104, 512, 512], P(None, None, 'chan', 'rad')
The draws below stay inside these ranges and needn't reach their ends.
Inputs may be any that keep to these rules, and one draw needn't show every extreme that they name: `slot_channel`: a permutation of the channel numbers; slot s belongs to group s // 26. Entries at positions counts[c] and beyond of a channel's lists are ignored.
All inputs are finite; a program needn't handle non-finite values.
Results may differ from the reference program's by a relative error of at most 0.0024.
Values may be sent and summed in bfloat16 or wider, within the bound.
No kernel may reach another device: no remote copies, remote signals or barrier semaphores. Data moves between devices by JAX's collectives and lax.ppermute only.
A program may use at most 192 MiB of HBM per device.

```python
import jax
import jax.numpy as jnp
from jax import lax

POINTS = 512
CHANNELS = 104
ORDERS = 4
LINKS = 12
VECTORS = 1
GROUP = 26


def draw_slot_channel(key, part):
    base = jax.random.fold_in(key, 11)
    order_key, inner_key = jax.random.split(base)
    groups = CHANNELS // GROUP
    group_order = jax.random.permutation(order_key, groups).astype(jnp.int32)
    scores = jax.random.randint(inner_key, (groups, GROUP), 0, 1 << 20) * GROUP + jnp.arange(GROUP, dtype=jnp.int32)[None, :]
    within = jnp.argsort(scores, axis=1).astype(jnp.int32)
    return (group_order[:, None] * GROUP + within).reshape(CHANNELS).astype(jnp.int32)


def draw_counts(key, part):
    noise = jax.random.randint(jax.random.fold_in(key, 5), (CHANNELS,), 0, 3)
    ids = jnp.arange(CHANNELS, dtype=jnp.int32)
    values = LINKS - ids * (LINKS - 2) // CHANNELS - noise
    values = jnp.clip(values, 1, LINKS)
    return jnp.where(ids == 0, LINKS, values).astype(jnp.int32)


def with_ends(result, own_key, least, largest):
    spot = [jax.random.randint(jax.random.fold_in(own_key, axis), (), 0, length) for axis, length in enumerate(result.shape)]
    widest = result.shape.index(max(result.shape))
    beside = spot[:widest] + [(spot[widest] + 1) % result.shape[widest]] + spot[widest + 1:]
    return result.at[tuple(spot)].set(least).at[tuple(beside)].set(largest)


def block_scale(key, extent, pieces, low, top_value):
    gain = 1.0
    for axis_at, blocks in pieces:
        heights = jax.random.uniform(jax.random.fold_in(jax.random.fold_in(key, 6), axis_at), (blocks,), jnp.float32, low / len(pieces), top_value / len(pieces))
        gain = gain * jnp.repeat(jnp.exp(heights), extent[axis_at] // blocks).reshape((-1,) + (1,) * (len(extent) - 1 - axis_at))
    return gain


def bell_draw(rng, shape, scale, bound, shards=(), kind=jnp.bfloat16):
    values = jax.random.normal(rng, shape, jnp.float32) * scale
    if len(shards) > 0:
        values = block_scale(rng, shape, shards, -0.22, 0.18) * values
    return jnp.clip(values, min=-bound, max=bound).astype(kind)


def setup_inputs(seed: int = 0) -> dict:
    streams_of = jax.random.split(jax.random.key(seed), 12)
    vectors = bell_draw(streams_of[0], (VECTORS, 2, CHANNELS, POINTS, POINTS), 1.0, 6.0, ((2, 4), (3, 8)), jnp.float32)
    eigenvectors = bell_draw(streams_of[1], (2, POINTS, POINTS), (2 * POINTS) ** -0.5, 0.1875, (), jnp.float32)
    energies = jnp.clip(jax.random.uniform(streams_of[2], (POINTS,), jnp.float32, 0.0, 2.0), 0.0, 2.0)
    widths = jnp.clip(jax.random.uniform(streams_of[3], (POINTS,), jnp.float32, 0.0, 1.0), 0.0, 1.0)
    shift_energy = jnp.clip(jax.random.uniform(streams_of[4], (1,), jnp.float32, 0.5, 2.0), 0.5, 2.0)
    shift_width = jnp.clip(jax.random.uniform(streams_of[5], (1,), jnp.float32, 0.5, 1.0), 0.5, 1.0)
    slot_channel = draw_slot_channel(jax.random.fold_in(streams_of[11], 71), 0)
    partners = with_ends(jax.random.randint(streams_of[7], (CHANNELS, LINKS), 0, CHANNELS), jax.random.fold_in(streams_of[7], 1), 0, CHANNELS - 1).astype(jnp.int32)
    multipole = with_ends(jax.random.randint(streams_of[8], (CHANNELS, LINKS), 0, ORDERS), jax.random.fold_in(streams_of[8], 1), 0, ORDERS - 1).astype(jnp.int32)
    counts = draw_counts(jax.random.fold_in(streams_of[11], 71), 0)
    angular = bell_draw(streams_of[10], (CHANNELS, LINKS), 2.0, 12.0, (), jnp.float32)
    return dict(vectors=vectors, eigenvectors=eigenvectors, energies=energies, widths=widths, shift_energy=shift_energy, shift_width=shift_width, slot_channel=slot_channel, partners=partners, multipole=multipole, counts=counts, angular=angular)


spacing = 0.01
first_point = 8.0
angle_ecs = 0.3
highest = lax.Precision.HIGHEST


def contour(index, points):
    start = (3 * points) // 4
    position = spacing * (index.astype(jnp.float32) + first_point)
    edge = spacing * (start + first_point)
    beyond = jnp.maximum(position - edge, 0.0)
    return (jnp.minimum(position, edge) + beyond * jnp.cos(angle_ecs), beyond * jnp.sin(angle_ecs))


def complex_product(first, second):
    return (first[0] * second[0] - first[1] * second[1], first[0] * second[1] + first[1] * second[0])


def kernels(row_index, col_index, points, orders):
    upper = contour(jnp.maximum(row_index[:, None], col_index[None, :]), points)
    lower = contour(jnp.minimum(row_index[:, None], col_index[None, :]), points)
    modulus = upper[0] * upper[0] + upper[1] * upper[1]
    inverse = (upper[0] / modulus, -upper[1] / modulus)
    ratio = complex_product(lower, inverse)
    real_list = [inverse[0]]
    imag_list = [inverse[1]]
    for order in range(1, orders):
        nextone = complex_product((real_list[-1], imag_list[-1]), ratio)
        real_list.append(nextone[0])
        imag_list.append(nextone[1])
    return (jnp.stack(real_list), jnp.stack(imag_list))


def transform(field, matrix, form):
    real_in = field[:, 0]
    imag_in = field[:, 1]
    out_real = jnp.einsum(form, real_in, matrix[0], precision=highest) - jnp.einsum(form, imag_in, matrix[1], precision=highest)
    out_imag = jnp.einsum(form, real_in, matrix[1], precision=highest) + jnp.einsum(form, imag_in, matrix[0], precision=highest)
    return jnp.stack([out_real, out_imag], axis=1)


def precondition(field, eigenvectors, factor):
    spectral = transform(field, eigenvectors, "nsra,ab->nsrb")
    spectral = transform(spectral, eigenvectors, "nsab,ai->nsib")
    scaled = jnp.stack(complex_product((spectral[:, 0], spectral[:, 1]), factor), axis=1)
    back = transform(scaled, eigenvectors, "nsib,ai->nsab")
    return transform(back, eigenvectors, "nsrb,ab->nsra")


def reference(vectors, eigenvectors, energies, widths, shift_energy, shift_width, slot_channel, partners, multipole, counts, angular):
    points = eigenvectors.shape[1]
    channels = slot_channel.shape[0]
    links = partners.shape[1]
    den_real = energies[:, None] + energies[None, :] - shift_energy[0]
    den_imag = -(widths[:, None] + widths[None, :]) - shift_width[0]
    modulus = den_real * den_real + den_imag * den_imag
    factor = (den_real / modulus, -den_imag / modulus)
    first = precondition(vectors, eigenvectors, factor)
    ids = jnp.arange(channels, dtype=jnp.int32)
    slot_of = jnp.zeros((channels,), jnp.int32).at[slot_channel].set(ids)
    live = jnp.arange(links, dtype=jnp.int32)[None, :] < counts[:, None]
    weight = jnp.where(live, angular, 0.0).astype(jnp.float32)
    target = jnp.broadcast_to(slot_of[:, None], (channels, links))
    source = slot_of[partners]
    coupling = jnp.zeros((ORDERS, channels, channels), jnp.float32).at[multipole, target, source].add(weight)
    coupled_in = lax.optimization_barrier(first.astype(jnp.bfloat16))
    widened = coupled_in.astype(jnp.float32)
    grid = jnp.arange(points, dtype=jnp.int32)
    table = kernels(grid, grid, points, ORDERS)
    total_real = jnp.zeros(first[:, 0].shape, jnp.float32)
    total_imag = jnp.zeros(first[:, 0].shape, jnp.float32)
    for order in range(ORDERS):
        mixed = jnp.einsum("st,nqtab->nqsab", coupling[order], widened, precision=highest)
        added = complex_product((table[0][order], table[1][order]), (mixed[:, 0], mixed[:, 1]))
        total_real = total_real + added[0]
        total_imag = total_imag + added[1]
    coupled = jnp.stack([total_real, total_imag], axis=1)
    return first - precondition(coupled, eigenvectors, factor)
```

```python
import functools

import jax
import jax.numpy as jnp
from jax import lax
from jax.experimental import pallas as pl
from jax.experimental.pallas import tpu as pltpu
from jax.sharding import PartitionSpec as P

ORDERS = 4
LANES = 128
GROUP_ROWS = 16

spacing = 0.01
first_point = 8.0
angle_ecs = 0.3

bf16 = jnp.bfloat16
f32 = jnp.float32
i16 = jnp.int16
i32 = jnp.int32
VMEM = pl.BlockSpec(memory_space=pltpu.VMEM)


def contour(index, points):
    start = 3 * points // 4
    position = spacing * (index.astype(f32) + first_point)
    edge = spacing * (start + first_point)
    beyond = jnp.maximum(position - edge, 0.0)
    return (jnp.minimum(position, edge) + beyond * jnp.cos(angle_ecs), beyond * jnp.sin(angle_ecs))


def complex_product(first, second):
    return (
        first[0] * second[0] - first[1] * second[1],
        first[0] * second[1] + first[1] * second[0],
    )


def exponent_of(block):
    top = jnp.max(jnp.max(jnp.abs(block), axis=1, keepdims=True), axis=0, keepdims=True)
    top = jnp.maximum(top, 1e-30)
    return jnp.ceil(jnp.log2(top * 1.0001))


def encode_piece(parts, store, tail):
    rows, points = parts[0].shape
    chunks = points // LANES
    groups = rows // GROUP_ROWS
    exponents = []
    for q in range(2):
        for g in range(groups):
            block = parts[q][g * GROUP_ROWS : (g + 1) * GROUP_ROWS]
            exponent = exponent_of(block)
            exponents.append(exponent)
            coded = jnp.round(block * jnp.exp2(15.0 - exponent)).astype(i32).astype(i16)
            for c in range(chunks):
                store((q * chunks + c) * rows + g * GROUP_ROWS, coded[:, c * LANES : (c + 1) * LANES])
    row_ids = lax.broadcasted_iota(i32, (GROUP_ROWS, LANES), 0)
    kept = jnp.zeros((GROUP_ROWS, LANES), f32)
    for at, exponent in enumerate(exponents):
        kept = jnp.where(row_ids == at, exponent, kept)
    store(tail, kept.astype(i32).astype(i16))


def decode_piece(load, rows, points, tail, put):
    chunks = points // LANES
    groups = rows // GROUP_ROWS
    scales = jnp.exp2(load(tail).astype(i32).astype(f32) - 15.0)
    for q in range(2):
        for g in range(groups):
            at = q * groups + g
            scale = scales[at : at + 1, :]
            for c in range(chunks):
                coded = load((q * chunks + c) * rows + g * GROUP_ROWS)
                put(q, g * GROUP_ROWS, c * LANES, coded.astype(i32).astype(f32) * scale)


def piece_rows(rows, points):
    return 2 * (points // LANES) * rows + GROUP_ROWS


def encode_kernel(live, x_ref, out_ref):
    tail = out_ref.shape[1] - GROUP_ROWS

    def store(row, value):
        out_ref[0, pl.ds(row, GROUP_ROWS), :] = value

    @pl.when(pl.program_id(0) < live)
    def _():
        encode_piece([x_ref[0, 0, 0], x_ref[0, 1, 0]], store, tail)

    @pl.when(pl.program_id(0) >= live)
    def _():
        out_ref[...] = jnp.zeros_like(out_ref)


def encode_round(vectors, start, rad):
    _, _, group, rows, points = vectors.shape
    live = min(rad, group - start)
    size = piece_rows(rows, points)
    return pl.pallas_call(
        functools.partial(encode_kernel, live),
        grid=(rad,),
        in_specs=[
            pl.BlockSpec((1, 2, 1, rows, points), lambda s: (0, 0, start + jnp.minimum(s, live - 1), 0, 0))
        ],
        out_specs=pl.BlockSpec((1, size, LANES), lambda s: (s, 0, 0)),
        out_shape=jax.ShapeDtypeStruct((rad, size, LANES), i16),
        cost_estimate=pl.CostEstimate(flops=0, bytes_accessed=6 * rad * size * LANES, transcendentals=0),
    )(vectors)


def decode_kernel(rows, points, in_ref, *refs):
    out_ref = refs[-1]
    tail = in_ref.shape[1] - GROUP_ROWS

    def load(row):
        return in_ref[0, pl.ds(row, GROUP_ROWS), :]

    def put(q, row, column, value):
        out_ref[0, q, 0, pl.ds(row, GROUP_ROWS), pl.ds(column, LANES)] = value

    decode_piece(load, rows, points, tail, put)


def decode_round(pieces, total, start, shape):
    _, _, group, rows, points = shape
    rad, size, _ = pieces.shape
    live = min(rad, group - start)
    operands = [pieces]
    in_specs = [pl.BlockSpec((1, size, LANES), lambda s: (s, 0, 0))]
    aliases = {}
    if total is not None:
        operands.append(total)
        in_specs.append(pl.BlockSpec(memory_space=pl.ANY))
        aliases = {1: 0}
    return pl.pallas_call(
        functools.partial(decode_kernel, rows, points),
        grid=(live,),
        in_specs=in_specs,
        out_specs=pl.BlockSpec((1, 2, 1, rows, points), lambda s: (0, 0, start + s, 0, 0)),
        out_shape=jax.ShapeDtypeStruct(shape, f32),
        input_output_aliases=aliases,
        cost_estimate=pl.CostEstimate(flops=0, bytes_accessed=6 * rad * size * LANES, transcendentals=0),
    )(*operands)


def split(value):
    high = value.astype(bf16)
    return high, (value - high.astype(f32)).astype(bf16)


def dot(a, b):
    return jnp.dot(a, b, preferred_element_type=f32)


def dot_right(value, matrix, at):
    high, low = split(value)
    return dot(high, matrix[at]) + (dot(low, matrix[at]) + dot(high, matrix[at + 1]))


def dot_left(matrix, at, value):
    high, low = split(value)
    return dot(matrix[at], high) + (dot(matrix[at], low) + dot(matrix[at + 1], high))


def times_right(x, matrix):
    k1 = dot_right(x[0] + x[1], matrix, 0)
    k2 = dot_right(x[0], matrix, 2)
    k3 = dot_right(x[1], matrix, 4)
    return k1 - k3, k1 + k2


def times_left(matrix, x):
    k1 = dot_left(matrix, 0, x[0] + x[1])
    k2 = dot_left(matrix, 2, x[0])
    k3 = dot_left(matrix, 4, x[1])
    return k1 - k3, k1 + k2


def precondition(x, u_ref, ut_ref, factor_ref):
    y = times_right(x, u_ref)
    y = times_left(ut_ref, y)
    y = complex_product(y, (factor_ref[0], factor_ref[1]))
    y = times_left(u_ref, y)
    return times_right(y, ut_ref)


def prepare_kernel(vec_ref, er_ref, ec_ref, wr_ref, wc_ref, shift_ref, u_ref, ut_ref, factor_ref):
    real, imag = vec_ref[0], vec_ref[1]
    for out, (r, i) in ((u_ref, (real, imag)), (ut_ref, (real.T, imag.T))):
        for at, value in enumerate((r, i - r, r + i)):
            high, low = split(value)
            out[2 * at] = high
            out[2 * at + 1] = low
    den_real = ec_ref[...] + er_ref[...] - shift_ref[0:1, 0:1]
    den_imag = -(wc_ref[...] + wr_ref[...]) - shift_ref[0:1, 1:2]
    modulus = den_real * den_real + den_imag * den_imag
    factor_ref[0] = den_real / modulus
    factor_ref[1] = -den_imag / modulus


def prepare(eigenvectors, energies, widths, shift_energy, shift_width):
    points = eigenvectors.shape[1]
    shift = jnp.concatenate([shift_energy, shift_width])[None, :]
    matrix = jax.ShapeDtypeStruct((6, points, points), bf16)
    return pl.pallas_call(
        prepare_kernel,
        in_specs=[VMEM] * 6,
        out_specs=[VMEM] * 3,
        out_shape=[matrix, matrix, jax.ShapeDtypeStruct((2, points, points), f32)],
        compiler_params=pltpu.CompilerParams(vmem_limit_bytes=40 << 20),
        cost_estimate=pl.CostEstimate(flops=0, bytes_accessed=24 * points * points, transcendentals=0),
    )(eigenvectors, energies[None, :], energies[:, None], widths[None, :], widths[:, None], shift)


def first_kernel(plan, x_ref, u_ref, ut_ref, factor_ref, first_ref, out_ref, x_scr):
    rad, chan, rows, points, column_cuts, height = plan
    tail = x_ref.shape[1] - GROUP_ROWS
    for p in range(rad):

        def load(row):
            return x_ref[p, pl.ds(row, GROUP_ROWS), :]

        def put(q, row, column, value):
            x_scr[q, pl.ds(p * rows + row, GROUP_ROWS), pl.ds(column, LANES)] = value

        decode_piece(load, rows, points, tail, put)
    y = precondition((x_scr[0], x_scr[1]), u_ref, ut_ref, factor_ref)
    for q in range(2):
        first_ref[q] = y[q]
        rounded = y[q].astype(bf16)
        for z in range(chan):
            column = (z % column_cuts) * LANES
            for p in range(rad):
                row = p * rows + (z // column_cuts) * height
                out_ref[z * rad + p, q] = rounded[row : row + height, column : column + LANES]


def p_cost(points, extra):
    return pl.CostEstimate(flops=36 * 2 * points**3, bytes_accessed=28 * points * points + extra, transcendentals=0)


def first_round(pieces, u, ut, factor, plan):
    rad, chan, rows, points, column_cuts, height = plan
    return pl.pallas_call(
        functools.partial(first_kernel, plan),
        in_specs=[VMEM] * 4,
        out_specs=[VMEM] * 2,
        out_shape=[
            jax.ShapeDtypeStruct((2, points, points), f32),
            jax.ShapeDtypeStruct((chan * rad, 2, height, LANES), bf16),
        ],
        scratch_shapes=[pltpu.VMEM((2, points, points), f32)],
        compiler_params=pltpu.CompilerParams(vmem_limit_bytes=40 << 20),
        cost_estimate=p_cost(points, 16 * points * points),
    )(pieces, u, ut, factor)


def second_kernel(plan, x_ref, first_ref, u_ref, ut_ref, factor_ref, out_ref, x_scr):
    rad, chan, rows, points, column_cuts, height = plan
    tail = out_ref.shape[1] - GROUP_ROWS
    for q in range(2):
        for z in range(chan):
            column = (z % column_cuts) * LANES
            for p in range(rad):
                row = p * rows + (z // column_cuts) * height
                x_scr[q, pl.ds(row, height), pl.ds(column, LANES)] = x_ref[z * rad + p, q].astype(f32)
    y = precondition((x_scr[0], x_scr[1]), u_ref, ut_ref, factor_ref)
    for q in range(2):
        x_scr[q] = first_ref[q] - y[q]
    for p in range(rad):

        def store(row, value):
            out_ref[p, pl.ds(row, GROUP_ROWS), :] = value

        encode_piece([x_scr[q, pl.ds(p * rows, rows), :] for q in range(2)], store, tail)


def second_round(pieces, first, u, ut, factor, plan):
    rad, chan, rows, points, column_cuts, height = plan
    size = piece_rows(rows, points)
    return pl.pallas_call(
        functools.partial(second_kernel, plan),
        in_specs=[VMEM] * 5,
        out_specs=VMEM,
        out_shape=jax.ShapeDtypeStruct((rad, size, LANES), i16),
        scratch_shapes=[pltpu.VMEM((2, points, points), f32)],
        compiler_params=pltpu.CompilerParams(vmem_limit_bytes=40 << 20),
        cost_estimate=p_cost(points, 16 * points * points),
    )(pieces, first, u, ut, factor)


def weights_kernel(row_ref, col_ref, partners_ref, multipole_ref, counts_ref, angular_ref, out_ref):
    channels, links = partners_ref.shape
    slots = row_ref.shape[1]
    ids = lax.broadcasted_iota(i32, (channels, channels), 1)
    rows_hot = (col_ref[...] == lax.broadcasted_iota(i32, (slots, channels), 1)).astype(f32)
    cols_hot = (row_ref[...] == lax.broadcasted_iota(i32, (channels, slots), 0)).astype(f32)
    tables = [jnp.zeros((channels, channels), f32) for _ in range(ORDERS)]
    for link in range(links):
        live = counts_ref[...] > link
        weight = jnp.where(live, angular_ref[:, link : link + 1], 0.0)
        spread = jnp.where(partners_ref[:, link : link + 1] == ids, weight, 0.0)
        order = multipole_ref[:, link : link + 1]
        for k in range(ORDERS):
            tables[k] = tables[k] + jnp.where(order == k, spread, 0.0)
    for k in range(ORDERS):
        sources = jnp.dot(tables[k], cols_hot, precision=lax.Precision.HIGHEST, preferred_element_type=f32)
        coupling = jnp.dot(rows_hot, sources, precision=lax.Precision.HIGHEST, preferred_element_type=f32)
        high, low = split(coupling)
        rounds, _, per, _ = out_ref.shape
        for j in range(rounds):
            out_ref[j, k, :, 0:slots] = high[j * per : (j + 1) * per]
            out_ref[j, k, :, slots : 2 * slots] = low[j * per : (j + 1) * per]


def coupling_weights(slot_channel, partners, multipole, counts, angular, chan, rad, rounds):
    group = slot_channel.shape[0] // chan
    arranged = jnp.pad(slot_channel.reshape(chan, group), ((0, 0), (0, rounds * rad - group)), constant_values=-1)
    arranged = arranged.reshape(chan, rounds, rad).transpose(1, 0, 2).reshape(-1)
    slots = arranged.shape[0]
    return pl.pallas_call(
        weights_kernel,
        in_specs=[VMEM] * 6,
        out_specs=VMEM,
        out_shape=jax.ShapeDtypeStruct((rounds, ORDERS, slots // rounds, 2 * slots), bf16),
    )(arranged[None, :], arranged[:, None], partners, multipole, counts[:, None], angular)


PACK = 4


def gather_kernel(*refs):
    out_ref, scr = refs[-2], refs[-1]
    rounds = len(refs) - 2
    per, _, height, _ = refs[0].shape
    for q in range(2):
        for j in range(rounds):
            for d in range(per):
                scr[pl.ds((j * per + d) * height, height), :] = refs[j][d, q].astype(f32)
        for r in range(height):
            value = scr[pl.ds(r, rounds * per, stride=height), :]
            out_ref[q, r // PACK, :, pl.ds((r % PACK) * LANES, LANES)] = value.astype(bf16)


def gather_slots(shared):
    per, _, height, _ = shared[0].shape
    slots = per * len(shared)
    return pl.pallas_call(
        gather_kernel,
        in_specs=[VMEM] * len(shared),
        out_specs=VMEM,
        out_shape=jax.ShapeDtypeStruct((2, height // PACK, slots, PACK * LANES), bf16),
        scratch_shapes=[pltpu.VMEM((slots * height, LANES), f32)],
        compiler_params=pltpu.CompilerParams(vmem_limit_bytes=40 << 20),
    )(*shared)


def couple_kernel(x_ref, weight_ref, table_ref, out_ref, scr):
    _, packs, slots, width = x_ref.shape
    per, _, height, _ = out_ref.shape
    weight = weight_ref[...].reshape(ORDERS * per, 2 * slots)

    def step(g, carry):
        mixed = []
        for q in range(2):
            value = x_ref[q, g]
            mixed.append(dot(weight, jnp.concatenate([value, value], axis=0)))
        inverse = (table_ref[0, pl.ds(g, 1), :], table_ref[1, pl.ds(g, 1), :])
        ratio = (table_ref[2, pl.ds(g, 1), :], table_ref[3, pl.ds(g, 1), :])
        total = [mixed[q][(ORDERS - 1) * per :] for q in range(2)]
        for k in range(ORDERS - 2, -1, -1):
            total = complex_product(total, ratio)
            total = [total[q] + mixed[q][k * per : (k + 1) * per] for q in range(2)]
        total = complex_product(total, inverse)
        for q in range(2):
            for r in range(PACK):
                scr[q, pl.ds(g * PACK + r, per, stride=height), :] = total[q][:, r * LANES : (r + 1) * LANES]
        return carry

    lax.fori_loop(0, packs, step, 0)
    for q in range(2):
        for d in range(per):
            out_ref[d, q] = scr[q, pl.ds(d * height, height), :].astype(bf16)


def couple_round(gathered, weight, table, height):
    _, packs, slots, width = gathered.shape
    per = weight.shape[1]
    return pl.pallas_call(
        couple_kernel,
        in_specs=[VMEM] * 3,
        out_specs=VMEM,
        out_shape=jax.ShapeDtypeStruct((per, 2, height, LANES), bf16),
        scratch_shapes=[pltpu.VMEM((2, per * height, LANES), f32)],
        compiler_params=pltpu.CompilerParams(vmem_limit_bytes=40 << 20),
        cost_estimate=pl.CostEstimate(
            flops=32 * packs * per * slots * width, bytes_accessed=6 << 20, transcendentals=0
        ),
    )(gathered, weight, table)


def kernel_table(row_ids, col_ids, points):
    upper = contour(jnp.maximum(row_ids[:, None], col_ids[None, :]), points)
    lower = contour(jnp.minimum(row_ids[:, None], col_ids[None, :]), points)
    modulus = upper[0] * upper[0] + upper[1] * upper[1]
    inverse = (upper[0] / modulus, -upper[1] / modulus)
    ratio = complex_product(lower, inverse)
    return jnp.stack([inverse[0], inverse[1], ratio[0], ratio[1]])


def local(
    vectors,
    eigenvectors,
    energies,
    widths,
    shift_energy,
    shift_width,
    slot_channel,
    partners,
    multipole,
    counts,
    angular,
):
    _, _, group, rows, points = vectors.shape
    chan = lax.axis_size("chan")
    rad = lax.axis_size("rad")
    rounds = -(-group // rad)
    column_cuts = min(chan, points // LANES)
    height = rows // (chan // column_cuts)
    plan = (rad, chan, rows, points, column_cuts, height)

    sent = [encode_round(vectors, j * rad, rad) for j in range(rounds)]
    u, ut, factor = prepare(eigenvectors, energies, widths, shift_energy, shift_width)
    weights = coupling_weights(slot_channel, partners, multipole, counts, angular, chan, rad, rounds)
    z = lax.axis_index("chan")
    row_ids = lax.axis_index("rad") * rows + (z // column_cuts) * height + jnp.arange(height, dtype=i32)
    col_ids = (z % column_cuts) * LANES + jnp.arange(LANES, dtype=i32)
    table = kernel_table(row_ids, col_ids, points).reshape(4, height // PACK, PACK * LANES)

    firsts, shared = [], []
    for j in range(rounds):
        mine = lax.all_to_all(sent[j], "rad", 0, 0, tiled=True)
        first, pieces = first_round(mine, u, ut, factor, plan)
        firsts.append(first)
        shared.append(lax.all_to_all(pieces, ("chan", "rad"), 0, 0, tiled=True))
    gathered = gather_slots(shared)
    total = None
    for j in range(rounds):
        coupled = couple_round(gathered, weights[j], table, height)
        mine = lax.all_to_all(coupled, ("chan", "rad"), 0, 0, tiled=True)
        update = second_round(mine, firsts[j], u, ut, factor, plan)
        pieces = lax.all_to_all(update, "rad", 0, 0, tiled=True)
        total = decode_round(pieces, total, j * rad, vectors.shape)
    return total


def solution(mesh):
    in_specs = (P(None, None, "chan", "rad", None),) + (P(),) * 10
    out_specs = P(None, None, "chan", "rad", None)
    return jax.shard_map(local, mesh=mesh, in_specs=in_specs, out_specs=out_specs, check_vma=False)
```

```python
import functools

import jax
import jax.numpy as jnp
from jax import lax
from jax.experimental import pallas as pl
from jax.experimental.pallas import tpu as pltpu
from jax.sharding import PartitionSpec as P

ORDERS = 4
LANES = 128
GROUP_ROWS = 16

spacing = 0.01
first_point = 8.0
angle_ecs = 0.3

bf16 = jnp.bfloat16
f32 = jnp.float32
i16 = jnp.int16
i32 = jnp.int32
VMEM = pl.BlockSpec(memory_space=pltpu.VMEM)
SMEM = pl.BlockSpec(memory_space=pltpu.SMEM)
ANY = pl.BlockSpec(memory_space=pl.ANY)
ROOM = pltpu.CompilerParams(vmem_limit_bytes=60 << 20)
LEAN = pltpu.CompilerParams(vmem_limit_bytes=20 << 20)


def contour(index, points):
    start = 3 * points // 4
    position = spacing * (index.astype(f32) + first_point)
    edge = spacing * (start + first_point)
    beyond = jnp.maximum(position - edge, 0.0)
    return (jnp.minimum(position, edge) + beyond * jnp.cos(angle_ecs), beyond * jnp.sin(angle_ecs))


def complex_product(first, second):
    return (
        first[0] * second[0] - first[1] * second[1],
        first[0] * second[1] + first[1] * second[0],
    )


def coded_parts(parts):
    rows, points = parts[0].shape
    groups = rows // GROUP_ROWS
    codes, exponents = [], []
    for part in parts:
        top = jnp.abs(part[:, 0:LANES])
        for c in range(1, points // LANES):
            top = jnp.maximum(top, jnp.abs(part[:, c * LANES : (c + 1) * LANES]))
        top = jnp.max(top.reshape(groups, GROUP_ROWS, LANES), axis=1)
        top = jnp.maximum(jnp.max(top, axis=1, keepdims=True), 1e-30)
        exponent = jnp.broadcast_to(jnp.ceil(jnp.log2(top * 1.0001)), (groups, LANES))
        scale = jnp.exp2(15.0 - exponent)
        scale = jnp.broadcast_to(scale[:, None, :], (groups, GROUP_ROWS, LANES)).reshape(rows, LANES)
        codes.append(
            [
                jnp.round(part[:, c * LANES : (c + 1) * LANES] * scale).astype(i32).astype(i16)
                for c in range(points // LANES)
            ]
        )
        exponents.append(exponent)
    return codes, exponents


def tail_of(exponents):
    used = sum(e.shape[0] for e in exponents)
    rest = [jnp.zeros((GROUP_ROWS - used, LANES), f32)] if used < GROUP_ROWS else []
    return jnp.concatenate(exponents + rest, axis=0).astype(i32).astype(i16)


def decode_piece(load, rows, points, put):
    chunks = points // LANES
    groups = rows // GROUP_ROWS
    scales = jnp.exp2(load(2 * chunks * rows).astype(i32).astype(f32) - 15.0)
    for q in range(2):
        for g in range(groups):
            at = q * groups + g
            scale = scales[at : at + 1, :]
            for c in range(chunks):
                coded = load((q * chunks + c) * rows + g * GROUP_ROWS)
                put(q, g * GROUP_ROWS, c * LANES, coded.astype(i32).astype(f32) * scale)


def piece_rows(rows, points):
    return 2 * (points // LANES) * rows + GROUP_ROWS


def slot_to(spot, live):
    return spot & (live - 1) if live & (live - 1) == 0 else spot


def encode_kernel(rounds, natural, spot_ref, *refs):
    xs, outs = refs[: len(rounds)], refs[len(rounds) :]
    rad = outs[0].shape[0] if natural else len(outs)
    for j, (_, live) in enumerate(rounds):
        rows, points = xs[j].shape[3:]
        chunks = points // LANES
        size = piece_rows(rows, points)
        for d in range(rad):
            out_ref = outs[0].at[d] if natural else outs[d]
            slot = slot_to(d if natural else spot_ref[0] ^ d, live)
            kept = jnp.where(slot < live, 1.0, 0.0)
            slot = jnp.minimum(slot, live - 1)
            codes, exponents = coded_parts([xs[j][0, q, slot] * kept for q in range(2)])
            for q in range(2):
                for c, code in enumerate(codes[q]):
                    out_ref[pl.ds(j * size + (q * chunks + c) * rows, rows), :] = code
            out_ref[pl.ds((j + 1) * size - GROUP_ROWS, GROUP_ROWS), :] = tail_of(exponents)


def encode_rounds(vectors, rounds, rad, spot, natural):
    _, _, group, rows, points = vectors.shape
    size = piece_rows(rows, points) * len(rounds)

    def block(start, live):
        return pl.BlockSpec((1, 2, live, rows, points), lambda i: (0, 0, start // live, 0, 0))

    if natural:
        shapes = [jax.ShapeDtypeStruct((rad, size, LANES), i16)]
    else:
        shapes = [jax.ShapeDtypeStruct((size, LANES), i16)] * rad
    return pl.pallas_call(
        functools.partial(encode_kernel, rounds, natural),
        grid=(1,),
        in_specs=[SMEM] + [block(*r) for r in rounds],
        out_specs=[VMEM] * len(shapes),
        out_shape=shapes,
        compiler_params=ROOM,
        cost_estimate=pl.CostEstimate(flops=0, bytes_accessed=6 * rad * size * LANES, transcendentals=0),
    )(spot, *[vectors for _ in rounds])


def decode_kernel(live, rows, points, spot_ref, *refs):
    out_ref = refs[-1]
    pieces = pieces_of(refs[:-2])
    for d, piece in enumerate(pieces):
        if len(refs) == 3 and d >= live:
            break
        slot = d if len(refs) == 3 else slot_to(spot_ref[0] ^ d, live)

        def write():
            def put(q, row, column, value):
                out_ref[0, q, slot, pl.ds(row, GROUP_ROWS), pl.ds(column, LANES)] = value

            decode_piece(lambda row: piece[pl.ds(row, GROUP_ROWS), :], rows, points, put)

        if len(refs) == 3 or live & (live - 1) == 0:
            write()
        else:
            pl.when(slot < live)(write)


def pieces_of(refs):
    return [refs[0].at[p] for p in range(refs[0].shape[0])] if len(refs) == 1 else list(refs)


def decode_round(pieces, total, start, live, spot, shape):
    _, _, _, rows, points = shape
    size = pieces[0].shape[-2]
    aliases = {} if total is None else {1 + len(pieces): 0}
    return pl.pallas_call(
        functools.partial(decode_kernel, live, rows, points),
        grid=(1,),
        in_specs=[SMEM] + [VMEM] * len(pieces) + [ANY],
        out_specs=pl.BlockSpec((1, 2, live, rows, points), lambda i: (0, 0, start // live, 0, 0)),
        out_shape=jax.ShapeDtypeStruct(shape, f32),
        input_output_aliases=aliases,
        compiler_params=ROOM,
        cost_estimate=pl.CostEstimate(flops=0, bytes_accessed=6 * live * size * LANES, transcendentals=0),
    )(spot, *pieces, spot if total is None else total)


def split(value):
    high = value.astype(bf16)
    return high, (value - high.astype(f32)).astype(bf16)


def dot(a, b):
    return jnp.dot(a, b, preferred_element_type=f32)


def dot_right(value, matrix, at):
    high, low = split(value)
    return dot(high, matrix[at]) + (dot(low, matrix[at]) + dot(high, matrix[at + 1]))


def dot_left(matrix, at, value):
    high, low = split(value)
    return dot(matrix[at], high) + (dot(matrix[at], low) + dot(matrix[at + 1], high))


def times_right(x, matrix):
    k1 = dot_right(x[0] + x[1], matrix, 0)
    k2 = dot_right(x[0], matrix, 2)
    k3 = dot_right(x[1], matrix, 4)
    return k1 - k3, k1 + k2


def times_left(matrix, x):
    k1 = dot_left(matrix, 0, x[0] + x[1])
    k2 = dot_left(matrix, 2, x[0])
    k3 = dot_left(matrix, 4, x[1])
    return k1 - k3, k1 + k2


def fetch(refs, held, sems):
    copies = [pltpu.make_async_copy(ref, scr, sems.at[i]) for i, (ref, scr) in enumerate(zip(refs, held))]
    for copy in copies:
        copy.start()
    return copies


def precondition(x, held, copies):
    u_ref, ut_ref, factor_ref = held[:3]
    copies[0].wait()
    y = times_right(x, u_ref)
    copies[1].wait()
    y = times_left(ut_ref, y)
    copies[2].wait()
    y = complex_product(y, (factor_ref[0], factor_ref[1]))
    y = times_left(u_ref, y)
    return times_right(y, ut_ref)


def p_scratch(points, count):
    matrix = pltpu.VMEM((6, points, points), bf16)
    field = pltpu.VMEM((2, points, points), f32)
    return [field, matrix, matrix] + [field] * (count - 2) + [pltpu.SemaphoreType.DMA((count,))]


def prepare_kernel(shift_energy_ref, shift_width_ref, vec_ref, energy_ref, width_ref, u_ref, ut_ref, factor_ref):
    real, imag = vec_ref[0], vec_ref[1]
    for out, (r, i) in ((u_ref, (real, imag)), (ut_ref, (real.T, imag.T))):
        for at, value in enumerate((r, i - r, r + i)):
            high, low = split(value)
            out[2 * at] = high
            out[2 * at + 1] = low
    energy = jnp.broadcast_to(energy_ref[...], real.shape)
    width = jnp.broadcast_to(width_ref[...], real.shape)
    den_real = energy.T + energy - shift_energy_ref[0]
    den_imag = -(width.T + width) - shift_width_ref[0]
    modulus = den_real * den_real + den_imag * den_imag
    factor_ref[0] = den_real / modulus
    factor_ref[1] = -den_imag / modulus


def prepare(eigenvectors, energies, widths, shift_energy, shift_width):
    points = eigenvectors.shape[1]
    matrix = jax.ShapeDtypeStruct((6, points, points), bf16)
    return pl.pallas_call(
        prepare_kernel,
        in_specs=[SMEM] * 2 + [VMEM] * 3,
        out_specs=[VMEM] * 3,
        out_shape=[matrix, matrix, jax.ShapeDtypeStruct((2, points, points), f32)],
        compiler_params=ROOM,
        cost_estimate=pl.CostEstimate(flops=0, bytes_accessed=24 * points * points, transcendentals=0),
    )(shift_energy, shift_width, eigenvectors, energies[None, :], widths[None, :])


def p_cost(points):
    return pl.CostEstimate(flops=36 * 2 * points**3, bytes_accessed=16 * points * points, transcendentals=0)


def fill_from_rows(refs, x_scr, me, rows, points):
    for d, piece in enumerate(pieces_of(refs)):
        base = d * rows if len(refs) == 1 else pl.multiple_of((me ^ d) * rows, rows)

        def put(q, row, column, value):
            x_scr[q, pl.ds(base + row, GROUP_ROWS), pl.ds(column, LANES)] = value

        decode_piece(lambda row: piece[pl.ds(row, GROUP_ROWS), :], rows, points, put)


def first_kernel(plan, shared, taken, spot_ref, *refs):
    rad, chan, rows, points, column_cuts, height = plan
    pieces, given = refs[:taken], refs[taken : taken + 3]
    first_ref, outs = refs[taken + 3], refs[taken + 4 : -5]
    x_scr, held, sems = refs[-5], refs[-4:-1], refs[-1]
    copies = fetch(given, held, sems)
    me, z_me = spot_ref[0], spot_ref[1]
    fill_from_rows(pieces, x_scr, me, rows, points)
    y = precondition((x_scr[0], x_scr[1]), held, copies)
    for q in range(2):
        first_ref[q] = y[q]
        if shared is None:
            rounded = y[q].astype(bf16)
            for z in range(chan):
                column = (z % column_cuts) * LANES
                for p in range(rad):
                    row = p * rows + (z // column_cuts) * height
                    outs[0][z * rad + p, q] = rounded[row : row + height, column : column + LANES]
        else:
            for d in range(shared):
                row = pl.multiple_of((me ^ d) * rows, rows)
                for e in range(chan):
                    column = pl.multiple_of((z_me ^ e) * LANES, LANES)
                    outs[d][e, q] = first_ref[q, pl.ds(row, height), pl.ds(column, LANES)].astype(bf16)


def first_round(pieces, at, u, ut, factor, spot, plan, shared=None):
    rad, chan, rows, points, column_cuts, height = plan
    size = piece_rows(rows, points)
    if len(pieces) == 1:
        block = [pl.BlockSpec((rad, size, LANES), lambda i: (0, at, 0))]
    else:
        block = [pl.BlockSpec((size, LANES), lambda i: (at, 0))] * rad
    if shared is None:
        sent = [jax.ShapeDtypeStruct((chan * rad, 2, height, LANES), bf16)]
    else:
        sent = [jax.ShapeDtypeStruct((chan, 2, height, LANES), bf16)] * shared
    result = pl.pallas_call(
        functools.partial(first_kernel, plan, shared, len(pieces)),
        grid=(1,),
        in_specs=[SMEM] + block + [ANY] * 3,
        out_specs=[VMEM] * (1 + len(sent)),
        out_shape=[jax.ShapeDtypeStruct((2, points, points), f32)] + sent,
        scratch_shapes=p_scratch(points, 3),
        compiler_params=ROOM,
        cost_estimate=p_cost(points),
    )(spot, *pieces, u, ut, factor)
    return result[0], result[1:]


def second_kernel(plan, shared, taken, spot_ref, *refs):
    rad, chan, rows, points, column_cuts, height = plan
    pieces, given, outs = refs[:taken], refs[taken : taken + 4], refs[taken + 4 : -8]
    code_scr, exp_scr, x_scr = refs[-8:-5]
    held, sems = refs[-5:-1], refs[-1]
    copies = fetch(given, held, sems)
    me, z_me = spot_ref[0], spot_ref[1]
    for q in range(2):
        if shared is None:
            for z in range(chan):
                column = (z % column_cuts) * LANES
                for p in range(rad):
                    row = p * rows + (z // column_cuts) * height
                    x_scr[q, pl.ds(row, height), pl.ds(column, LANES)] = pieces[0][z * rad + p, q].astype(f32)
        else:
            for d in range(rad):
                row = pl.multiple_of((me ^ d) * rows, rows)
                for e in range(chan):
                    column = pl.multiple_of((z_me ^ e) * LANES, LANES)
                    x_scr[q, pl.ds(row, height), pl.ds(column, LANES)] = pieces[d][e, q].astype(f32)
    y = precondition((x_scr[0], x_scr[1]), held, copies)
    copies[3].wait()
    codes, exponents = coded_parts([held[3][q] - y[q] for q in range(2)])
    groups = rows // GROUP_ROWS
    for q in range(2):
        for c, code in enumerate(codes[q]):
            code_scr[q, c] = code
        for p in range(rad):
            exp_scr[p, pl.ds(q * groups, groups), :] = exponents[q][p * groups : (p + 1) * groups]
    chunks = points // LANES
    for d, out_ref in enumerate(pieces_of(outs)):
        spot = d if len(outs) == 1 else me ^ d
        row = d * rows if len(outs) == 1 else pl.multiple_of(spot * rows, rows)
        for q in range(2):
            for c in range(chunks):
                out_ref[pl.ds((q * chunks + c) * rows, rows), :] = code_scr[q, c, pl.ds(row, rows), :]
        out_ref[pl.ds(2 * chunks * rows, GROUP_ROWS), :] = tail_of([exp_scr[spot]])


def tail_rows(rows):
    return 2 * (rows // GROUP_ROWS)


def second_round(pieces, first, u, ut, factor, spot, plan, shared=None, natural=False):
    rad, chan, rows, points, column_cuts, height = plan
    size = piece_rows(rows, points)
    if natural:
        shapes = [jax.ShapeDtypeStruct((rad, size, LANES), i16)]
    else:
        shapes = [jax.ShapeDtypeStruct((size, LANES), i16)] * (rad if shared is None else shared)
    return pl.pallas_call(
        functools.partial(second_kernel, plan, shared, len(pieces)),
        in_specs=[SMEM] + [VMEM] * len(pieces) + [ANY] * 4,
        out_specs=[VMEM] * len(shapes),
        out_shape=shapes,
        scratch_shapes=[
            pltpu.VMEM((2, points // LANES, points, LANES), i16),
            pltpu.VMEM((rad, tail_rows(rows), LANES), f32),
        ]
        + p_scratch(points, 4),
        compiler_params=ROOM,
        cost_estimate=p_cost(points),
    )(spot, *pieces, u, ut, factor, first)


def weights_kernel(layout, channel_ref, partners_ref, multipole_ref, counts_ref, angular_ref, out_ref):
    chan, rad, full, live = layout
    links, channels = partners_ref.shape
    slots = out_ref.shape[1]
    group = channels // chan
    exact = dict(precision=lax.Precision.HIGHEST, preferred_element_type=f32)
    last = (((1,), (1,)), ((), ()))

    def ids(shape, axis):
        return lax.broadcasted_iota(i32, shape, axis)

    at, slot = ids((slots, channels), 0), ids((slots, channels), 1)
    z, inner = slot // group, slot % group
    found = (inner // rad) * (chan * rad) + z * rad + inner % rad
    if live:
        found = jnp.where(inner < full * rad, found, full * chan * rad + z * live + inner - full * rad)
    place = (at == found).astype(f32)
    held = (channel_ref[...] == ids((channels, channels), 0)).astype(f32)
    hot = lax.dot_general(place, held, last, **exact)
    tables = [jnp.zeros((channels, channels), f32) for _ in range(ORDERS)]
    for link in range(links):
        row = slice(link, link + 1)
        weight = jnp.where(counts_ref[...] > link, angular_ref[row, :], 0.0)
        spread = jnp.where(partners_ref[row, :] == ids((channels, channels), 0), weight, 0.0)
        for k in range(ORDERS):
            tables[k] = tables[k] + jnp.where(multipole_ref[row, :] == k, spread, 0.0)
    for k in range(ORDERS):
        targets = lax.dot_general(hot, tables[k], last, **exact)
        coupling = lax.dot_general(targets, hot, last, **exact)
        high, low = split(coupling)
        out_ref[k, :, 0:slots] = high
        out_ref[k, :, slots : 2 * slots] = low


def coupling_weights(slot_channel, partners, multipole, counts, angular, layout):
    chan, rad, full, live = layout
    slots = (full + (live > 0)) * chan * rad
    return pl.pallas_call(
        functools.partial(weights_kernel, layout),
        in_specs=[VMEM] * 5,
        out_specs=VMEM,
        out_shape=jax.ShapeDtypeStruct((ORDERS, slots, 2 * slots), bf16),
        compiler_params=ROOM,
        cost_estimate=pl.CostEstimate(flops=0, bytes_accessed=8 << 20, transcendentals=0),
    )(slot_channel[None, :], partners.T, multipole.T, counts[None, :], angular.T)


PACK = 4


def gather_kernel(shared, spot_ref, *refs):
    out_ref, scr = refs[-2], refs[-1]
    per = out_ref.shape[2]
    height = scr.shape[0] // per
    for q in range(2):
        if shared is None:
            for d in range(per):
                scr[pl.ds(d * height, height), :] = refs[0][d, q].astype(f32)
        else:
            scr[...] = jnp.zeros_like(scr)
            for e, ref in enumerate(refs[:-2]):
                for d in range(shared):
                    at = (spot_ref[1] ^ e) * shared + ((spot_ref[0] ^ d) & (shared - 1))
                    scr[pl.ds(pl.multiple_of(at * height, height), height), :] = ref[d, q].astype(f32)
        for r in range(height):
            value = scr[pl.ds(r, per, stride=height), :]
            out_ref[q, r // PACK, :, pl.ds((r % PACK) * LANES, LANES)] = value.astype(bf16)


def gather_round(pieces, spot, per, shared=None):
    height = pieces[0].shape[2]
    return pl.pallas_call(
        functools.partial(gather_kernel, shared),
        in_specs=[SMEM] + [VMEM] * len(pieces),
        out_specs=VMEM,
        out_shape=jax.ShapeDtypeStruct((2, height // PACK, per, PACK * LANES), bf16),
        scratch_shapes=[pltpu.VMEM((per * height, LANES), f32)],
        compiler_params=LEAN,
        cost_estimate=pl.CostEstimate(flops=0, bytes_accessed=8 * per * height * LANES, transcendentals=0),
    )(spot, *pieces)


def couple_kernel(sources, at, per, shared, spot_ref, weight_ref, table_ref, *refs):
    xs, scr = refs[:sources], refs[-1]
    outs = refs[sources:-1]
    packs = xs[0].shape[1]
    height = packs * PACK
    weight = weight_ref[:, at : at + per, :].reshape(ORDERS * per, weight_ref.shape[2])

    def step(g, carry):
        mixed = []
        for q in range(2):
            values = [x[q, g] for x in xs]
            mixed.append(dot(weight, jnp.concatenate(values + values, axis=0)))
        inverse = (table_ref[0, pl.ds(g, 1), :], table_ref[1, pl.ds(g, 1), :])
        ratio = (table_ref[2, pl.ds(g, 1), :], table_ref[3, pl.ds(g, 1), :])
        total = [mixed[q][(ORDERS - 1) * per :] for q in range(2)]
        for k in range(ORDERS - 2, -1, -1):
            total = complex_product(total, ratio)
            total = [total[q] + mixed[q][k * per : (k + 1) * per] for q in range(2)]
        total = complex_product(total, inverse)
        for q in range(2):
            for r in range(PACK):
                scr[q, pl.ds(g * PACK + r, per, stride=height), :] = total[q][:, r * LANES : (r + 1) * LANES]
        return carry

    lax.fori_loop(0, packs, step, 0, unroll=2)
    for q in range(2):
        if shared is None:
            for d in range(per):
                outs[0][d, q] = scr[q, pl.ds(d * height, height), :].astype(bf16)
        else:
            for e, out_ref in enumerate(outs):
                for d in range(shared):
                    slot = (spot_ref[1] ^ e) * shared + ((spot_ref[0] ^ d) & (shared - 1))
                    row = pl.multiple_of(slot * height, height)
                    out_ref[d, q] = scr[q, pl.ds(row, height), :].astype(bf16)


def couple_round(gathered, weights, table, spot, at, chan, per, shared=None):
    _, packs, _, width = gathered[0].shape
    height = packs * PACK
    slots = weights.shape[2]
    if shared is None:
        outs = [jax.ShapeDtypeStruct((per, 2, height, LANES), bf16)]
    else:
        outs = [jax.ShapeDtypeStruct((shared, 2, height, LANES), bf16)] * chan
    return pl.pallas_call(
        functools.partial(couple_kernel, len(gathered), at, per, shared),
        in_specs=[SMEM] + [VMEM] * (2 + len(gathered)),
        out_specs=[VMEM] * len(outs),
        out_shape=outs,
        scratch_shapes=[pltpu.VMEM((2, per * height, LANES), f32)],
        compiler_params=LEAN,
        cost_estimate=pl.CostEstimate(
            flops=32 * packs * per * slots * width, bytes_accessed=6 << 20, transcendentals=0
        ),
    )(spot, weights, table, *gathered)


def kernel_table(row_ids, col_ids, points):
    upper = contour(jnp.maximum(row_ids[:, None], col_ids[None, :]), points)
    lower = contour(jnp.minimum(row_ids[:, None], col_ids[None, :]), points)
    modulus = upper[0] * upper[0] + upper[1] * upper[1]
    inverse = (upper[0] / modulus, -upper[1] / modulus)
    ratio = complex_product(lower, inverse)
    return jnp.stack([inverse[0], inverse[1], ratio[0], ratio[1]])


def local(
    vectors,
    eigenvectors,
    energies,
    widths,
    shift_energy,
    shift_width,
    slot_channel,
    partners,
    multipole,
    counts,
    angular,
):
    _, _, group, rows, points = vectors.shape
    chan = lax.axis_size("chan")
    rad = lax.axis_size("rad")
    column_cuts = min(chan, points // LANES)
    height = rows // (chan // column_cuts)
    plan = (rad, chan, rows, points, column_cuts, height)
    full, live = group // rad, group % rad
    if live & (live - 1) or column_cuts != chan:
        full, live = full + 1, 0
    spot = jnp.stack([lax.axis_index("rad"), lax.axis_index("chan")]).astype(i32)

    def over_rad(pieces):
        return [pieces[0]] + [
            lax.ppermute(piece, "rad", [(i, i ^ d) for i in range(rad)]) for d, piece in enumerate(pieces) if d
        ]

    def over_chan(pieces):
        return [pieces[0]] + [
            lax.ppermute(piece, "chan", [(i, i ^ e) for i in range(chan)]) for e, piece in enumerate(pieces) if e
        ]

    def over_all(piece):
        return lax.all_to_all(piece, ("chan", "rad"), 0, 0, tiled=True)

    rounds = [(j * rad, min(rad, group - j * rad)) for j in range(full)]
    if live:
        rounds.append((full * rad, live))
    everyone = chan * rad
    cut = lax.optimization_barrier

    def share(piece):
        return lax.all_to_all(piece, "rad", 0, 0, tiled=True)

    near = [encode_rounds(vectors, [r], rad, spot, True)[0] for r in rounds[:2]]
    far = encode_rounds(vectors, rounds[2:], rad, spot, False) if rounds[2:] else []
    u, ut, factor = prepare(eigenvectors, energies, widths, shift_energy, shift_width)
    received, near, far, u, ut, factor, small = cut(
        (share(near[0]), near, far, u, ut, factor, (slot_channel, partners, multipole, counts, angular, spot))
    )

    def apply_first(pieces, at, shared=None):
        return first_round(pieces, at, u, ut, factor, spot, plan, shared)

    firsts, gathered = [], []
    first, pieces = apply_first([received], 0)
    firsts.append(first)
    received = share(near[1]) if len(near) > 1 else received
    flying, received, small, far = cut((pieces[0], received, small, far))
    received = ([received], 0)
    for j in range(1, len(rounds)):
        flying = over_all(flying)
        if j == 1 and far:
            arriving = over_rad(far)
        first, pieces = apply_first(*received, live if j == full else None)
        firsts.append(first)
        if j == 1 and j < full:
            flown, pieces, small, arriving = cut((flying, pieces, small, arriving if far else ()))
        elif j < full:
            flown, pieces = cut((flying, pieces))
        else:
            others = [
                lax.ppermute(piece, "rad", [(i, i ^ d) for i in range(rad)]) for d, piece in enumerate(pieces) if d
            ]
            pieces = [pieces[0]] + others
            pieces = over_chan([jnp.stack([piece[e] for piece in pieces]) for e in range(chan)])
            flown, pieces = cut((flying, pieces))
        received = (arriving, j - 1) if far else None
        flying = pieces[0]
        gathered.append(gather_round([flown], spot, everyone))
    if not live:
        gathered.append(gather_round([over_all(flying)], spot, everyone))
    weights = coupling_weights(*small[:5], (chan, rad, full, live))
    z = lax.axis_index("chan")
    row_ids = lax.axis_index("rad") * rows + (z // column_cuts) * height + jnp.arange(height, dtype=i32)
    col_ids = (z % column_cuts) * LANES + jnp.arange(LANES, dtype=i32)
    table = kernel_table(row_ids, col_ids, points).reshape(4, height // PACK, PACK * LANES)
    if live:
        gathered.append(gather_round(pieces, spot, everyone, live))

    def couple(j):
        if j == full:
            return couple_round(gathered, weights, table, spot, full * everyone, chan, chan * live, live)
        return couple_round(gathered, weights, table, spot, j * everyone, chan, everyone)[0]

    def apply_second(pieces, j, shared=None):
        return second_round(pieces, firsts[j], u, ut, factor, spot, plan, shared, shared is None and j >= full - 2)

    def give(update):
        return [share(update[0])] if len(update) == 1 else over_rad(update)

    coupled, gathered, firsts = cut((couple(0), gathered, firsts))
    update, shared, total, ready = None, None, None, []
    for j in range(full):
        flown = over_all(coupled)
        ahead = couple(j + 1) if j + 1 < full else coupled
        if live and j == 0:
            shared = over_chan(couple(full))
        if live and j == min(1, full - 1):
            shared = [jnp.stack([piece[d] for piece in shared]) for d in range(live)]
            shared = over_rad([shared[d % live] for d in range(rad)])
        if update is not None:
            ready.append(over_rad(update) if len(update) > 1 else update)
        update = apply_second([mine], j - 1) if j > 0 else None
        mine, coupled, update, gathered, ready, shared = cut((flown, ahead, update, gathered, ready, shared))
    if update is not None:
        ready.append(give(update))
    update = apply_second([mine], full - 1)
    update, ready, shared = cut((update, ready, shared))
    done = give(update)
    for j, pieces in enumerate(ready):
        total = decode_round(pieces, total, *rounds[j], spot, vectors.shape)
    if live:
        extra = apply_second(shared, full, live)
        done, extra, total = cut((done, extra, total))
        extra = over_rad(extra)
    total = decode_round(done, total, *rounds[full - 1], spot, vectors.shape)
    if live:
        total = decode_round(extra, total, *rounds[full], spot, vectors.shape)
    return total


def solution(mesh):
    in_specs = (P(None, None, "chan", "rad", None),) + (P(),) * 10
    out_specs = P(None, None, "chan", "rad", None)
    return jax.shard_map(local, mesh=mesh, in_specs=in_specs, out_specs=out_specs, check_vma=False)
```

```python
import functools

import jax
import jax.numpy as jnp
from jax import lax
from jax.experimental import pallas as pl
from jax.experimental.pallas import tpu as pltpu
from jax.sharding import PartitionSpec as P

ORDERS = 4
LANES = 128
GROUP_ROWS = 16

spacing = 0.01
first_point = 8.0
angle_ecs = 0.3

bf16 = jnp.bfloat16
f32 = jnp.float32
i16 = jnp.int16
i32 = jnp.int32
VMEM = pl.BlockSpec(memory_space=pltpu.VMEM)
SMEM = pl.BlockSpec(memory_space=pltpu.SMEM)
ANY = pl.BlockSpec(memory_space=pl.ANY)
ROOM = pltpu.CompilerParams(vmem_limit_bytes=60 << 20)
LEAN = pltpu.CompilerParams(vmem_limit_bytes=20 << 20)


def contour(index, points):
    start = 3 * points // 4
    position = spacing * (index.astype(f32) + first_point)
    edge = spacing * (start + first_point)
    beyond = jnp.maximum(position - edge, 0.0)
    return (jnp.minimum(position, edge) + beyond * jnp.cos(angle_ecs), beyond * jnp.sin(angle_ecs))


def complex_product(first, second):
    return (
        first[0] * second[0] - first[1] * second[1],
        first[0] * second[1] + first[1] * second[0],
    )


def coded_parts(parts):
    rows, points = parts[0].shape
    groups = rows // GROUP_ROWS
    codes, exponents = [], []
    for part in parts:
        top = jnp.abs(part[:, 0:LANES])
        for c in range(1, points // LANES):
            top = jnp.maximum(top, jnp.abs(part[:, c * LANES : (c + 1) * LANES]))
        top = jnp.max(top.reshape(groups, GROUP_ROWS, LANES), axis=1)
        top = jnp.maximum(jnp.max(top, axis=1, keepdims=True), 1e-30)
        exponent = jnp.broadcast_to(jnp.ceil(jnp.log2(top * 1.0001)), (groups, LANES))
        scale = jnp.exp2(15.0 - exponent)
        scale = jnp.broadcast_to(scale[:, None, :], (groups, GROUP_ROWS, LANES)).reshape(rows, LANES)
        codes.append(
            [
                jnp.round(part[:, c * LANES : (c + 1) * LANES] * scale).astype(i32).astype(i16)
                for c in range(points // LANES)
            ]
        )
        exponents.append(exponent)
    return codes, exponents


def tail_of(exponents):
    used = sum(e.shape[0] for e in exponents)
    rest = [jnp.zeros((GROUP_ROWS - used, LANES), f32)] if used < GROUP_ROWS else []
    return jnp.concatenate(exponents + rest, axis=0).astype(i32).astype(i16)


def decode_piece(load, rows, points, put):
    chunks = points // LANES
    groups = rows // GROUP_ROWS
    scales = jnp.exp2(load(2 * chunks * rows).astype(i32).astype(f32) - 15.0)
    for q in range(2):
        for g in range(groups):
            at = q * groups + g
            scale = scales[at : at + 1, :]
            for c in range(chunks):
                coded = load((q * chunks + c) * rows + g * GROUP_ROWS)
                put(q, g * GROUP_ROWS, c * LANES, coded.astype(i32).astype(f32) * scale)


def piece_rows(rows, points):
    return 2 * (points // LANES) * rows + GROUP_ROWS


def slot_to(spot, live):
    return spot & (live - 1) if live & (live - 1) == 0 else spot


def encode_kernel(rounds, natural, spot_ref, *refs):
    xs, outs = refs[: len(rounds)], refs[len(rounds) :]
    rad = outs[0].shape[0] if natural else 2 * len(outs)
    for j, (_, live) in enumerate(rounds):
        rows, points = xs[j].shape[3:]
        chunks = points // LANES
        size = piece_rows(rows, points)
        for d in range(rad):
            out_ref = outs[0].at[d] if natural else outs[d // 2]
            base = j * size if natural else ((d % 2) * len(rounds) + j) * size
            slot = slot_to(d if natural else spot_ref[0] ^ d, live)
            kept = jnp.where(slot < live, 1.0, 0.0)
            slot = jnp.minimum(slot, live - 1)
            codes, exponents = coded_parts([xs[j][0, q, slot] * kept for q in range(2)])
            for q in range(2):
                for c, code in enumerate(codes[q]):
                    out_ref[pl.ds(base + (q * chunks + c) * rows, rows), :] = code
            out_ref[pl.ds(base + size - GROUP_ROWS, GROUP_ROWS), :] = tail_of(exponents)


def encode_rounds(vectors, rounds, rad, spot, natural):
    _, _, group, rows, points = vectors.shape
    size = piece_rows(rows, points) * len(rounds)

    def block(start, live):
        return pl.BlockSpec((1, 2, live, rows, points), lambda i: (0, 0, start // live, 0, 0))

    if natural:
        shapes = [jax.ShapeDtypeStruct((rad, size, LANES), i16)]
    else:
        shapes = [jax.ShapeDtypeStruct((2 * size, LANES), i16)] * (rad // 2)
    return pl.pallas_call(
        functools.partial(encode_kernel, rounds, natural),
        grid=(1,),
        in_specs=[SMEM] + [block(*r) for r in rounds],
        out_specs=[VMEM] * len(shapes),
        out_shape=shapes,
        compiler_params=ROOM,
        cost_estimate=pl.CostEstimate(flops=0, bytes_accessed=6 * rad * size * LANES, transcendentals=0),
    )(spot, *[vectors for _ in rounds])


def halves_kernel(*refs):
    sources, out_ref, sems = refs[:-2], refs[-2], refs[-1]
    half = sources[0].shape[0] // 2
    copies = [
        pltpu.make_async_copy(ref.at[pl.ds(half, half)], out_ref.at[pl.ds(i * half, half)], sems.at[i])
        for i, ref in enumerate(sources)
    ]
    for copy in copies:
        copy.start()
    for copy in copies:
        copy.wait()


def second_halves(arrays):
    shape = arrays[0].shape
    return pl.pallas_call(
        halves_kernel,
        in_specs=[ANY] * len(arrays),
        out_specs=VMEM,
        out_shape=jax.ShapeDtypeStruct((len(arrays) * (shape[0] // 2),) + shape[1:], arrays[0].dtype),
        scratch_shapes=[pltpu.SemaphoreType.DMA((len(arrays),))],
        compiler_params=ROOM,
        cost_estimate=pl.CostEstimate(flops=0, bytes_accessed=4 << 20, transcendentals=0),
    )(*arrays)


class Pieces:
    def __init__(self, blocks, natural):
        self.blocks = blocks
        self.natural = natural

    def arrays(self):
        return [array for array, _ in self.blocks]

    def specs(self, lead):
        def spec(array, number):
            rest = array.shape[1:]
            return pl.BlockSpec((lead,) + rest, lambda i: (number,) + (0,) * len(rest))

        return [spec(array, number) for array, number in self.blocks]

    def views(self, refs, lead):
        return [ref.at[pl.ds(number * lead, lead)] for ref, (_, number) in zip(refs, self.blocks)]

    def place(self, at, me):
        return at if self.natural else me ^ at


def decode_kernel(live, rows, points, pieces, spot_ref, *refs):
    out_ref = refs[-1]
    for d, piece in enumerate(refs[:-2]):
        slot = slot_to(pieces.place(d, spot_ref[0]), live)

        def write():
            def put(q, row, column, value):
                out_ref[0, q, slot, pl.ds(row, GROUP_ROWS), pl.ds(column, LANES)] = value

            decode_piece(lambda row: piece[pl.ds(row, GROUP_ROWS), :], rows, points, put)

        if live & (live - 1) == 0:
            write()
        elif d < live:
            write()


def decode_round(pieces, total, start, live, spot, shape):
    _, _, _, rows, points = shape
    size = piece_rows(rows, points)
    count = len(pieces.blocks)
    aliases = {} if total is None else {1 + count: 0}
    return pl.pallas_call(
        functools.partial(decode_kernel, live, rows, points, pieces),
        grid=(1,),
        in_specs=[SMEM] + pieces.specs(size) + [ANY],
        out_specs=pl.BlockSpec((1, 2, live, rows, points), lambda i: (0, 0, start // live, 0, 0)),
        out_shape=jax.ShapeDtypeStruct(shape, f32),
        input_output_aliases=aliases,
        compiler_params=ROOM,
        cost_estimate=pl.CostEstimate(flops=0, bytes_accessed=6 * live * size * LANES, transcendentals=0),
    )(spot, *pieces.arrays(), spot if total is None else total)


def split(value):
    high = value.astype(bf16)
    return high, (value - high.astype(f32)).astype(bf16)


def dot(a, b):
    return jnp.dot(a, b, preferred_element_type=f32)


def dot_right(value, matrix, at):
    high, low = split(value)
    return dot(high, matrix[at]) + (dot(low, matrix[at]) + dot(high, matrix[at + 1]))


def dot_left(matrix, at, value):
    high, low = split(value)
    return dot(matrix[at], high) + (dot(matrix[at], low) + dot(matrix[at + 1], high))


def times_right(x, matrix, ready=(), finish=None):
    for copy in ready[:1]:
        copy.wait()
    k1 = dot_right(x[0] + x[1], matrix, 0)
    for copy in ready[1:2]:
        copy.wait()
    k3 = dot_right(x[1], matrix, 4)
    real = k1 - k3
    if finish is not None:
        finish(0, real)
    for copy in ready[2:]:
        copy.wait()
    k2 = dot_right(x[0], matrix, 2)
    if finish is not None:
        finish(1, k1 + k2)
    return real, k1 + k2


def times_left(matrix, x):
    k1 = dot_left(matrix, 0, x[0] + x[1])
    k2 = dot_left(matrix, 2, x[0])
    k3 = dot_left(matrix, 4, x[1])
    return k1 - k3, k1 + k2


class Copies:
    def __init__(self, sems):
        self.sems = sems
        self.count = 0

    def start(self, source, target):
        copy = pltpu.make_async_copy(source, target, self.sems.at[self.count])
        self.count += 1
        copy.start()
        return copy


def precondition(x_scr, given, held, copies, fill, finish, last=None):
    u_ref, ut_ref, factor_ref = held[:3]
    ready = [copies.start(given[0].at[pl.ds(at, 2)], u_ref.at[pl.ds(at, 2)]) for at in (0, 4, 2)]
    copy = copies.start(given[1], ut_ref)
    scaling = copies.start(given[2], factor_ref)
    fill()
    y = times_right((x_scr[0], x_scr[1]), u_ref, ready)
    copy.wait()
    y = times_left(ut_ref, y)
    scaling.wait()
    if last is not None:
        last()
    y = complex_product(y, (factor_ref[0], factor_ref[1]))
    y = times_left(u_ref, y)
    times_right(y, ut_ref, (), finish)


def p_scratch(points, count, pieces):
    matrix = pltpu.VMEM((6, points, points), bf16)
    field = pltpu.VMEM((2, points, points), f32)
    return [field, matrix, matrix] + [field] * (count - 2) + [pltpu.SemaphoreType.DMA((pieces + 8,))]


def prepare_kernel(shift_energy_ref, shift_width_ref, vec_ref, energy_ref, width_ref, u_ref, ut_ref, factor_ref):
    real, imag = vec_ref[0], vec_ref[1]
    for out, (r, i) in ((u_ref, (real, imag)), (ut_ref, (real.T, imag.T))):
        for at, value in enumerate((r, i - r, r + i)):
            high, low = split(value)
            out[2 * at] = high
            out[2 * at + 1] = low
    points = real.shape[0]

    def both(ref):
        column = jnp.broadcast_to(ref[...], (LANES, points)).T
        return jnp.concatenate([column] * (points // LANES), axis=1) + ref[...]

    den_real = both(energy_ref) - shift_energy_ref[0]
    den_imag = -both(width_ref) - shift_width_ref[0]
    modulus = den_real * den_real + den_imag * den_imag
    factor_ref[0] = den_real / modulus
    factor_ref[1] = -den_imag / modulus


def prepare(eigenvectors, energies, widths, shift_energy, shift_width):
    points = eigenvectors.shape[1]
    matrix = jax.ShapeDtypeStruct((6, points, points), bf16)
    return pl.pallas_call(
        prepare_kernel,
        in_specs=[SMEM] * 2 + [VMEM] * 3,
        out_specs=[VMEM] * 3,
        out_shape=[matrix, matrix, jax.ShapeDtypeStruct((2, points, points), f32)],
        compiler_params=ROOM,
        cost_estimate=pl.CostEstimate(flops=0, bytes_accessed=24 * points * points, transcendentals=0),
    )(shift_energy, shift_width, eigenvectors, energies[None, :], widths[None, :])


def p_cost(points):
    return pl.CostEstimate(flops=36 * 2 * points**3, bytes_accessed=16 * points * points, transcendentals=0)


def fill_from_rows(pieces, refs, x_scr, me, rows, points):
    for d, piece in enumerate(refs):
        base = pieces.place(d, me) * rows
        if not pieces.natural:
            base = pl.multiple_of(base, rows)

        def put(q, row, column, value):
            x_scr[q, pl.ds(base + row, GROUP_ROWS), pl.ds(column, LANES)] = value

        decode_piece(lambda row: piece[pl.ds(row, GROUP_ROWS), :], rows, points, put)


def first_kernel(plan, shared, pieces, spot_ref, *refs):
    rad, chan, rows, points, column_cuts, height = plan
    given, first_ref, outs = refs[rad : rad + 3], refs[rad + 3], refs[rad + 4 : -6]
    in_scr, x_scr, held, sems = refs[-6], refs[-5], refs[-4:-1], refs[-1]
    me, z_me = spot_ref[0], spot_ref[1]
    copies = Copies(sems)
    views = pieces.views(refs[:rad], piece_rows(rows, points))
    arriving = [copies.start(view, in_scr.at[p]) for p, view in enumerate(views)]
    leaving = []

    def fill():
        for copy in arriving:
            copy.wait()
        fill_from_rows(pieces, [in_scr.at[p] for p in range(rad)], x_scr, me, rows, points)

    def finish(q, value):
        x_scr[q] = value
        leaving.append(copies.start(x_scr.at[q], first_ref.at[q]))
        if shared is None:
            rounded = value.astype(bf16)
            for z in range(chan):
                column = (z % column_cuts) * LANES
                for p in range(rad):
                    row = p * rows + (z // column_cuts) * height
                    outs[0][z * rad + p, q] = rounded[row : row + height, column : column + LANES]
        else:
            for d in range(shared):
                row = pl.multiple_of((me ^ d) * rows, rows)
                for e in range(chan):
                    column = pl.multiple_of((z_me ^ e) * LANES, LANES)
                    outs[d][e, q] = x_scr[q, pl.ds(row, height), pl.ds(column, LANES)].astype(bf16)

    precondition(x_scr, given, held, copies, fill, finish)
    for copy in leaving:
        copy.wait()


def first_round(pieces, u, ut, factor, spot, plan, shared=None):
    rad, chan, rows, points, column_cuts, height = plan
    size = piece_rows(rows, points)
    if shared is None:
        sent = [jax.ShapeDtypeStruct((chan * rad, 2, height, LANES), bf16)]
    else:
        sent = [jax.ShapeDtypeStruct((chan, 2, height, LANES), bf16)] * shared
    result = pl.pallas_call(
        functools.partial(first_kernel, plan, shared, pieces),
        in_specs=[SMEM] + [ANY] * (rad + 3),
        out_specs=[ANY] + [VMEM] * len(sent),
        out_shape=[jax.ShapeDtypeStruct((2, points, points), f32)] + sent,
        scratch_shapes=[pltpu.VMEM((rad, size, LANES), i16)] + p_scratch(points, 3, rad),
        compiler_params=ROOM,
        cost_estimate=p_cost(points),
    )(spot, *pieces.arrays(), u, ut, factor)
    return result[0], result[1:]


def second_kernel(plan, shared, natural, pieces, spot_ref, *refs):
    rad, chan, rows, points, column_cuts, height = plan
    taken = 1 if shared is None else rad
    given, outs = refs[taken : taken + 4], refs[taken + 4 : -9]
    in_scr, code_scr, exp_scr, x_scr = refs[-9:-5]
    held, sems = refs[-5:-1], refs[-1]
    me, z_me = spot_ref[0], spot_ref[1]
    copies = Copies(sems)
    if shared is None:
        arriving = [copies.start(refs[0], in_scr)]
    else:
        views = pieces.views(refs[:rad], chan)
        arriving = [copies.start(view, in_scr.at[pl.ds(d * chan, chan)]) for d, view in enumerate(views)]
    groups = rows // GROUP_ROWS
    kept = []

    def fill():
        for copy in arriving:
            copy.wait()
        for q in range(2):
            if shared is None:
                for z in range(chan):
                    column = (z % column_cuts) * LANES
                    for p in range(rad):
                        row = p * rows + (z // column_cuts) * height
                        x_scr[q, pl.ds(row, height), pl.ds(column, LANES)] = in_scr[z * rad + p, q].astype(f32)
            else:
                for d in range(rad):
                    row = pl.multiple_of((me ^ d) * rows, rows)
                    for e in range(chan):
                        column = pl.multiple_of((z_me ^ e) * LANES, LANES)
                        x_scr[q, pl.ds(row, height), pl.ds(column, LANES)] = in_scr[d * chan + e, q].astype(f32)

    def last():
        kept.append(copies.start(given[3], held[3]))

    def finish(q, value):
        if q == 0:
            kept[0].wait()
        codes, exponents = coded_parts([held[3][q] - value])
        for c, code in enumerate(codes[0]):
            code_scr[q, c] = code
        for p in range(rad):
            exp_scr[p, pl.ds(q * groups, groups), :] = exponents[0][p * groups : (p + 1) * groups]

    precondition(x_scr, given, held, copies, fill, finish, last)
    chunks = points // LANES
    size = piece_rows(rows, points)
    for d in range(rad if shared is None else shared):
        spot = d if natural else me ^ d
        row = d * rows if natural else pl.multiple_of(spot * rows, rows)
        if natural:
            out_ref, base = outs[0], d * size
        elif shared is None:
            out_ref, base = outs[d // 2], (d % 2) * size
        else:
            out_ref, base = outs[d], 0
        for q in range(2):
            for c in range(chunks):
                out_ref[pl.ds(base + (q * chunks + c) * rows, rows), :] = code_scr[q, c, pl.ds(row, rows), :]
        out_ref[pl.ds(base + 2 * chunks * rows, GROUP_ROWS), :] = tail_of([exp_scr[spot]])


def tail_rows(rows):
    return 2 * (rows // GROUP_ROWS)


def second_round(pieces, first, u, ut, factor, spot, plan, shared=None, natural=False):
    rad, chan, rows, points, column_cuts, height = plan
    size = piece_rows(rows, points)
    if natural:
        shapes = [jax.ShapeDtypeStruct((rad * size, LANES), i16)]
    elif shared is None:
        shapes = [jax.ShapeDtypeStruct((2 * size, LANES), i16)] * (rad // 2)
    else:
        shapes = [jax.ShapeDtypeStruct((size, LANES), i16)] * shared
    given = [pieces] if shared is None else pieces.arrays()
    return pl.pallas_call(
        functools.partial(second_kernel, plan, shared, natural, pieces),
        in_specs=[SMEM] + [ANY] * (len(given) + 4),
        out_specs=[VMEM] * len(shapes),
        out_shape=shapes,
        scratch_shapes=[
            pltpu.VMEM((chan * rad, 2, height, LANES), bf16),
            pltpu.VMEM((2, points // LANES, points, LANES), i16),
            pltpu.VMEM((rad, tail_rows(rows), LANES), f32),
        ]
        + p_scratch(points, 4, len(given)),
        compiler_params=ROOM,
        cost_estimate=p_cost(points),
    )(spot, *given, u, ut, factor, first)


def weights_kernel(layout, channel_ref, partners_ref, multipole_ref, counts_ref, angular_ref, out_ref):
    chan, rad, full, live = layout
    links, channels = partners_ref.shape
    slots = out_ref.shape[1]
    group = channels // chan
    exact = dict(precision=lax.Precision.HIGHEST, preferred_element_type=f32)
    last = (((1,), (1,)), ((), ()))

    def ids(shape, axis):
        return lax.broadcasted_iota(i32, shape, axis)

    at, slot = ids((slots, channels), 0), ids((slots, channels), 1)
    z, inner = slot // group, slot % group
    found = (inner // rad) * (chan * rad) + z * rad + inner % rad
    if live:
        found = jnp.where(inner < full * rad, found, full * chan * rad + z * live + inner - full * rad)
    place = (at == found).astype(f32)
    held = (channel_ref[...] == ids((channels, channels), 0)).astype(f32)
    hot = lax.dot_general(place, held, last, **exact)
    tables = [jnp.zeros((channels, channels), f32) for _ in range(ORDERS)]
    for link in range(links):
        row = slice(link, link + 1)
        weight = jnp.where(counts_ref[...] > link, angular_ref[row, :], 0.0)
        spread = jnp.where(partners_ref[row, :] == ids((channels, channels), 0), weight, 0.0)
        for k in range(ORDERS):
            tables[k] = tables[k] + jnp.where(multipole_ref[row, :] == k, spread, 0.0)
    for k in range(ORDERS):
        targets = lax.dot_general(hot, tables[k], last, **exact)
        coupling = lax.dot_general(targets, hot, last, **exact)
        high, low = split(coupling)
        out_ref[k, :, 0:slots] = high
        out_ref[k, :, slots : 2 * slots] = low


def coupling_weights(slot_channel, partners, multipole, counts, angular, layout):
    chan, rad, full, live = layout
    slots = (full + (live > 0)) * chan * rad
    return pl.pallas_call(
        functools.partial(weights_kernel, layout),
        in_specs=[VMEM] * 5,
        out_specs=VMEM,
        out_shape=jax.ShapeDtypeStruct((ORDERS, slots, 2 * slots), bf16),
        compiler_params=ROOM,
        cost_estimate=pl.CostEstimate(flops=0, bytes_accessed=8 << 20, transcendentals=0),
    )(slot_channel[None, :], partners.T, multipole.T, counts[None, :], angular.T)


PACK = 4


def gather_kernel(shared, spot_ref, *refs):
    out_ref, scr = refs[-2], refs[-1]
    per = out_ref.shape[2]
    height = scr.shape[0] // per
    for q in range(2):
        if shared is None:
            for d in range(per):
                scr[pl.ds(d * height, height), :] = refs[0][d, q].astype(f32)
        else:
            scr[...] = jnp.zeros_like(scr)
            for e, ref in enumerate(refs[:-2]):
                for d in range(shared):
                    at = (spot_ref[1] ^ e) * shared + ((spot_ref[0] ^ d) & (shared - 1))
                    scr[pl.ds(pl.multiple_of(at * height, height), height), :] = ref[d, q].astype(f32)
        for r in range(height):
            value = scr[pl.ds(r, per, stride=height), :]
            out_ref[q, r // PACK, :, pl.ds((r % PACK) * LANES, LANES)] = value.astype(bf16)


def gather_round(pieces, spot, per, shared=None):
    height = pieces[0].shape[2]
    return pl.pallas_call(
        functools.partial(gather_kernel, shared),
        in_specs=[SMEM] + [VMEM] * len(pieces),
        out_specs=VMEM,
        out_shape=jax.ShapeDtypeStruct((2, height // PACK, per, PACK * LANES), bf16),
        scratch_shapes=[pltpu.VMEM((per * height, LANES), f32)],
        compiler_params=LEAN,
        cost_estimate=pl.CostEstimate(flops=0, bytes_accessed=8 * per * height * LANES, transcendentals=0),
    )(spot, *pieces)


def couple_kernel(sources, at, per, shared, spot_ref, weight_ref, table_ref, *refs):
    xs, scr = refs[:sources], refs[-1]
    outs = refs[sources:-1]
    packs = xs[0].shape[1]
    height = packs * PACK
    weight = weight_ref[:, at : at + per, :].reshape(ORDERS * per, weight_ref.shape[2])

    def step(g, carry):
        mixed = []
        for q in range(2):
            values = [x[q, g] for x in xs]
            mixed.append(dot(weight, jnp.concatenate(values + values, axis=0)))
        inverse = (table_ref[0, pl.ds(g, 1), :], table_ref[1, pl.ds(g, 1), :])
        ratio = (table_ref[2, pl.ds(g, 1), :], table_ref[3, pl.ds(g, 1), :])
        total = [mixed[q][(ORDERS - 1) * per :] for q in range(2)]
        for k in range(ORDERS - 2, -1, -1):
            total = complex_product(total, ratio)
            total = [total[q] + mixed[q][k * per : (k + 1) * per] for q in range(2)]
        total = complex_product(total, inverse)
        for q in range(2):
            for r in range(PACK):
                scr[q, pl.ds(g * PACK + r, per, stride=height), :] = total[q][:, r * LANES : (r + 1) * LANES]
        return carry

    lax.fori_loop(0, packs, step, 0, unroll=2)
    for q in range(2):
        if shared is None:
            for d in range(per):
                outs[0][d, q] = scr[q, pl.ds(d * height, height), :].astype(bf16)
        else:
            for e, out_ref in enumerate(outs):
                for d in range(shared):
                    slot = (spot_ref[1] ^ e) * shared + ((spot_ref[0] ^ d) & (shared - 1))
                    row = pl.multiple_of(slot * height, height)
                    out_ref[d, q] = scr[q, pl.ds(row, height), :].astype(bf16)


def couple_round(gathered, weights, table, spot, at, chan, per, shared=None):
    _, packs, _, width = gathered[0].shape
    height = packs * PACK
    slots = weights.shape[2]
    if shared is None:
        outs = [jax.ShapeDtypeStruct((per, 2, height, LANES), bf16)]
    else:
        outs = [jax.ShapeDtypeStruct((shared, 2, height, LANES), bf16)] * chan
    return pl.pallas_call(
        functools.partial(couple_kernel, len(gathered), at, per, shared),
        in_specs=[SMEM] + [VMEM] * (2 + len(gathered)),
        out_specs=[VMEM] * len(outs),
        out_shape=outs,
        scratch_shapes=[pltpu.VMEM((2, per * height, LANES), f32)],
        compiler_params=LEAN,
        cost_estimate=pl.CostEstimate(
            flops=32 * packs * per * slots * width, bytes_accessed=6 << 20, transcendentals=0
        ),
    )(spot, weights, table, *gathered)


def kernel_table(row_ids, col_ids, points):
    upper = contour(jnp.maximum(row_ids[:, None], col_ids[None, :]), points)
    lower = contour(jnp.minimum(row_ids[:, None], col_ids[None, :]), points)
    modulus = upper[0] * upper[0] + upper[1] * upper[1]
    inverse = (upper[0] / modulus, -upper[1] / modulus)
    ratio = complex_product(lower, inverse)
    return jnp.stack([inverse[0], inverse[1], ratio[0], ratio[1]])


def local(
    vectors,
    eigenvectors,
    energies,
    widths,
    shift_energy,
    shift_width,
    slot_channel,
    partners,
    multipole,
    counts,
    angular,
):
    _, _, group, rows, points = vectors.shape
    chan = lax.axis_size("chan")
    rad = lax.axis_size("rad")
    column_cuts = min(chan, points // LANES)
    height = rows // (chan // column_cuts)
    plan = (rad, chan, rows, points, column_cuts, height)
    full, live = group // rad, group % rad
    if live != 2 or column_cuts != chan:
        full, live = full + 1, 0
    spot = jnp.stack([lax.axis_index("rad"), lax.axis_index("chan")]).astype(i32)

    def over(piece, axis, size, d):
        return lax.ppermute(piece, axis, [(i, i ^ d) for i in range(size)])

    def over_even(arrays):
        return [arrays[0]] + [over(array, "rad", rad, 2 * e) for e, array in enumerate(arrays) if e]

    def over_next(got, count):
        half = got[0].shape[0] // 2
        swapped = over(second_halves(got), "rad", rad, 1)
        return [
            Pieces([(swapped, (d // 2) * count + j) if d % 2 else (got[d // 2], j) for d in range(rad)], False)
            for j in range(count)
        ]

    def over_chan(pieces):
        return [pieces[0]] + [over(piece, "chan", chan, e) for e, piece in enumerate(pieces) if e]

    def over_all(piece):
        return lax.all_to_all(piece, ("chan", "rad"), 0, 0, tiled=True)

    def share(piece):
        flat = lax.all_to_all(piece.reshape(rad, -1, LANES), "rad", 0, 0, tiled=True).reshape(-1, LANES)
        return Pieces([(flat, p) for p in range(rad)], True)

    rounds = [(j * rad, min(rad, group - j * rad)) for j in range(full)]
    if live:
        rounds.append((full * rad, live))
    everyone = chan * rad

    def cut(values):
        is_pieces = lambda v: isinstance(v, Pieces)
        leaves, tree = jax.tree.flatten(values, is_leaf=is_pieces)
        arrays = {}
        for leaf in leaves:
            for array in leaf.arrays() if is_pieces(leaf) else [leaf]:
                arrays[id(array)] = array
        tied = dict(zip(arrays, lax.optimization_barrier(list(arrays.values()))))
        leaves = [
            Pieces([(tied[id(array)], at) for array, at in leaf.blocks], leaf.natural)
            if is_pieces(leaf)
            else tied[id(leaf)]
            for leaf in leaves
        ]
        return jax.tree.unflatten(tree, leaves)

    near = [encode_rounds(vectors, [r], rad, spot, True)[0] for r in rounds[:2]]
    far = [encode_rounds(vectors, [r], rad, spot, False) for r in rounds[2:3]]
    u, ut, factor = prepare(eigenvectors, energies, widths, shift_energy, shift_width)
    small = (slot_channel, partners, multipole, counts, angular, spot)
    received, near, far, u, ut, factor, small, later = cut((share(near[0]), near, far, u, ut, factor, small, vectors))

    def apply_first(pieces, shared=None):
        return first_round(pieces, u, ut, factor, spot, plan, shared)

    def constants(small):
        weights = coupling_weights(*small[:5], (chan, rad, full, live))
        z = small[5][1]
        row_ids = small[5][0] * rows + (z // column_cuts) * height + jnp.arange(height, dtype=i32)
        col_ids = (z % column_cuts) * LANES + jnp.arange(LANES, dtype=i32)
        return weights, kernel_table(row_ids, col_ids, points).reshape(4, height // PACK, PACK * LANES)

    firsts, gathered, arriving, fixed = [], [], (), None
    first, pieces = apply_first(received)
    firsts.append(first)
    if len(near) > 1:
        received = share(near[1])
    flying, received, small, far, later = cut((pieces[0], received, small, far, later))
    for j in range(1, len(rounds)):
        flying = over_all(flying)
        if j > 1:
            received = over_next(arriving, 1)[0]
        arriving = over_even(far[j - 1]) if j - 1 < len(far) else ()
        if j == 1:
            far += [encode_rounds(later, [r], rad, spot, False) for r in rounds[3:]]
        if j == 2:
            fixed = constants(small)
        first, pieces = apply_first(received, live if j == full else None)
        firsts.append(first)
        if j == full:
            pieces = [pieces[0]] + [over(piece, "rad", rad, d) for d, piece in enumerate(pieces) if d]
            pieces = over_chan([jnp.stack([piece[e] for piece in pieces]) for e in range(chan)])
        flown, pieces, small, far, arriving, gathered, fixed = cut(
            (flying, pieces, small, far, arriving, gathered, fixed)
        )
        flying = pieces[0]
        gathered.append(gather_round([flown], spot, everyone))
    if not live:
        gathered.append(gather_round([over_all(flying)], spot, everyone))
    weights, table = fixed or constants(small)
    if live:
        gathered.append(gather_round(pieces, spot, everyone, live))

    def couple(j):
        if j == full:
            return couple_round(gathered, weights, table, spot, full * everyone, chan, chan * live, live)
        return couple_round(gathered, weights, table, spot, j * everyone, chan, everyone)[0]

    def apply_second(pieces, j, shared=None):
        return second_round(pieces, firsts[j], u, ut, factor, spot, plan, shared, shared is None and j >= full - 2)

    coupled, gathered, firsts = cut((couple(0), gathered, firsts))
    coupled = [coupled]
    update, shared, total, ready = None, None, None, []
    for j in range(full):
        flown = over_all(coupled[j])
        if j == 0:
            coupled += [couple(k) for k in range(1, full)]
            shared = over_chan(couple(full)) if live else None
        if live and j == min(1, full - 1):
            both = jnp.concatenate([jnp.stack([piece[d] for piece in shared]) for d in range(live)])
            shared = over_even([both] * (rad // 2))
        elif live and j == min(2, full - 1):
            shared = over_next(shared, 1)[0]
        if j > 2:
            ready[j - 3] = over_next(ready[j - 3], 1)[0]
        if update is not None:
            ready.append(over_even(update) if len(update) > 1 else update)
        update = apply_second(mine, j - 1) if j > 0 else None
        mine, coupled, update, ready, shared = cut((flown, coupled, update, ready, shared))
    ready = [over_next(got, 1)[0] if isinstance(got, list) else got for got in ready]
    if live and full < 3:
        shared = over_next(shared, 1)[0]
    if update is not None:
        ready.append(share(update[0]))
    update = apply_second(mine, full - 1)
    update, ready, shared = cut((update, ready, shared))
    done = share(update[0])
    for j, pieces in enumerate(ready):
        total = decode_round(pieces, total, *rounds[j], spot, vectors.shape)
    if live:
        extra = apply_second(shared, full, live)
        done, extra, total = cut((done, extra, total))
        extra = [extra[0]] + [over(piece, "rad", rad, d) for d, piece in enumerate(extra) if d]
        extra = Pieces([(piece, 0) for piece in extra], False)
    total = decode_round(done, total, *rounds[full - 1], spot, vectors.shape)
    if live:
        total = decode_round(extra, total, *rounds[full], spot, vectors.shape)
    return total


def solution(mesh):
    in_specs = (P(None, None, "chan", "rad", None),) + (P(),) * 10
    out_specs = P(None, None, "chan", "rad", None)
    return jax.shard_map(local, mesh=mesh, in_specs=in_specs, out_specs=out_specs, check_vma=False)
```

```python
import functools

import jax
import jax.numpy as jnp
from jax import lax
from jax.experimental import pallas as pl
from jax.experimental.pallas import tpu as pltpu
from jax.sharding import PartitionSpec as P

ORDERS = 4
LANES = 128
GROUP_ROWS = 16

spacing = 0.01
first_point = 8.0
angle_ecs = 0.3

bf16 = jnp.bfloat16
f32 = jnp.float32
i16 = jnp.int16
i32 = jnp.int32
VMEM = pl.BlockSpec(memory_space=pltpu.VMEM)
SMEM = pl.BlockSpec(memory_space=pltpu.SMEM)
ANY = pl.BlockSpec(memory_space=pl.ANY)
ROOM = pltpu.CompilerParams(vmem_limit_bytes=60 << 20)
LEAN = pltpu.CompilerParams(vmem_limit_bytes=20 << 20)


def contour(index, points):
    start = 3 * points // 4
    position = spacing * (index.astype(f32) + first_point)
    edge = spacing * (start + first_point)
    beyond = jnp.maximum(position - edge, 0.0)
    return (jnp.minimum(position, edge) + beyond * jnp.cos(angle_ecs), beyond * jnp.sin(angle_ecs))


def complex_product(first, second):
    return (
        first[0] * second[0] - first[1] * second[1],
        first[0] * second[1] + first[1] * second[0],
    )


def coded_parts(parts):
    rows, points = parts[0].shape
    groups = rows // GROUP_ROWS
    codes, exponents = [], []
    for part in parts:
        top = jnp.abs(part[:, 0:LANES])
        for c in range(1, points // LANES):
            top = jnp.maximum(top, jnp.abs(part[:, c * LANES : (c + 1) * LANES]))
        top = jnp.max(top.reshape(groups, GROUP_ROWS, LANES), axis=1)
        top = jnp.maximum(jnp.max(top, axis=1, keepdims=True), 1e-30)
        exponent = jnp.broadcast_to(jnp.ceil(jnp.log2(top * 1.0001)), (groups, LANES))
        scale = jnp.exp2(15.0 - exponent)
        scale = jnp.broadcast_to(scale[:, None, :], (groups, GROUP_ROWS, LANES)).reshape(rows, LANES)
        codes.append(
            [
                jnp.round(part[:, c * LANES : (c + 1) * LANES] * scale).astype(i32).astype(i16)
                for c in range(points // LANES)
            ]
        )
        exponents.append(exponent)
    return codes, exponents


def tail_of(exponents):
    used = sum(e.shape[0] for e in exponents)
    rest = [jnp.zeros((GROUP_ROWS - used, LANES), f32)] if used < GROUP_ROWS else []
    return jnp.concatenate(exponents + rest, axis=0).astype(i32).astype(i16)


def decode_piece(load, rows, points, put):
    chunks = points // LANES
    groups = rows // GROUP_ROWS
    scales = jnp.exp2(load(2 * chunks * rows).astype(i32).astype(f32) - 15.0)
    for q in range(2):
        for g in range(groups):
            at = q * groups + g
            scale = scales[at : at + 1, :]
            for c in range(chunks):
                coded = load((q * chunks + c) * rows + g * GROUP_ROWS)
                put(q, g * GROUP_ROWS, c * LANES, coded.astype(i32).astype(f32) * scale)


def piece_rows(rows, points):
    return 2 * (points // LANES) * rows + GROUP_ROWS


def slot_to(spot, live):
    return spot & (live - 1) if live & (live - 1) == 0 else spot


def encode_kernel(rounds, natural, spot_ref, *refs):
    xs, outs = refs[: len(rounds)], refs[len(rounds) :]
    rad = outs[0].shape[0] if natural else 2 * len(outs)
    for j, (_, live) in enumerate(rounds):
        rows, points = xs[j].shape[3:]
        chunks = points // LANES
        size = piece_rows(rows, points)
        for d in range(rad):
            out_ref = outs[0].at[d] if natural else outs[d // 2]
            base = j * size if natural else ((d % 2) * len(rounds) + j) * size
            slot = slot_to(d if natural else spot_ref[0] ^ d, live)
            kept = jnp.where(slot < live, 1.0, 0.0)
            slot = jnp.minimum(slot, live - 1)
            codes, exponents = coded_parts([xs[j][0, q, slot] * kept for q in range(2)])
            for q in range(2):
                for c, code in enumerate(codes[q]):
                    out_ref[pl.ds(base + (q * chunks + c) * rows, rows), :] = code
            out_ref[pl.ds(base + size - GROUP_ROWS, GROUP_ROWS), :] = tail_of(exponents)


def encode_rounds(vectors, rounds, rad, spot, natural):
    _, _, group, rows, points = vectors.shape
    size = piece_rows(rows, points) * len(rounds)

    def block(start, live):
        return pl.BlockSpec((1, 2, live, rows, points), lambda i: (0, 0, start // live, 0, 0))

    if natural:
        shapes = [jax.ShapeDtypeStruct((rad, size, LANES), i16)]
    else:
        shapes = [jax.ShapeDtypeStruct((2 * size, LANES), i16)] * (rad // 2)
    return pl.pallas_call(
        functools.partial(encode_kernel, rounds, natural),
        grid=(1,),
        in_specs=[SMEM] + [block(*r) for r in rounds],
        out_specs=[VMEM] * len(shapes),
        out_shape=shapes,
        compiler_params=ROOM,
        cost_estimate=pl.CostEstimate(flops=0, bytes_accessed=6 * rad * size * LANES, transcendentals=0),
    )(spot, *[vectors for _ in rounds])


def halves_kernel(*refs):
    sources, out_ref, sems = refs[:-2], refs[-2], refs[-1]
    half = sources[0].shape[0] // 2
    copies = [
        pltpu.make_async_copy(ref.at[pl.ds(half, half)], out_ref.at[pl.ds(i * half, half)], sems.at[i])
        for i, ref in enumerate(sources)
    ]
    for copy in copies:
        copy.start()
    for copy in copies:
        copy.wait()


def second_halves(arrays):
    shape = arrays[0].shape
    return pl.pallas_call(
        halves_kernel,
        in_specs=[ANY] * len(arrays),
        out_specs=VMEM,
        out_shape=jax.ShapeDtypeStruct((len(arrays) * (shape[0] // 2),) + shape[1:], arrays[0].dtype),
        scratch_shapes=[pltpu.SemaphoreType.DMA((len(arrays),))],
        compiler_params=ROOM,
        cost_estimate=pl.CostEstimate(flops=0, bytes_accessed=4 << 20, transcendentals=0),
    )(*arrays)


class Pieces:
    def __init__(self, blocks, natural):
        self.blocks = blocks
        self.natural = natural

    def arrays(self):
        return [array for array, _ in self.blocks]

    def specs(self, lead):
        def spec(array, number):
            rest = array.shape[1:]
            return pl.BlockSpec((lead,) + rest, lambda i: (number,) + (0,) * len(rest))

        return [spec(array, number) for array, number in self.blocks]

    def views(self, refs, lead):
        return [ref.at[pl.ds(number * lead, lead)] for ref, (_, number) in zip(refs, self.blocks)]

    def place(self, at, me):
        return at if self.natural else me ^ at


def decode_kernel(lives, rows, points, given, spot_ref, *refs):
    out_ref = refs[-1]
    first, base = 0, 0
    for live, pieces in zip(lives, given):
        for d in range(len(pieces.blocks)):
            piece = refs[first + d]
            slot = base + slot_to(pieces.place(d, spot_ref[0]), live)

            def write():
                def put(q, row, column, value):
                    out_ref[0, q, slot, pl.ds(row, GROUP_ROWS), pl.ds(column, LANES)] = value

                decode_piece(lambda row: piece[pl.ds(row, GROUP_ROWS), :], rows, points, put)

            if live & (live - 1) == 0:
                write()
            elif d < live:
                write()
        first, base = first + len(pieces.blocks), base + live


def decode_rounds(given, total, rounds, spot, shape):
    _, _, _, rows, points = shape
    size = piece_rows(rows, points)
    arrays = [array for pieces in given for array in pieces.arrays()]
    specs = [spec for pieces in given for spec in pieces.specs(size)]
    start, lives = rounds[0][0], [live for _, live in rounds]
    count = sum(lives)
    aliases = {} if total is None else {1 + len(arrays): 0}
    return pl.pallas_call(
        functools.partial(decode_kernel, lives, rows, points, given),
        grid=(1,),
        in_specs=[SMEM] + specs + [ANY],
        out_specs=pl.BlockSpec((1, 2, count, rows, points), lambda i: (0, 0, start // count, 0, 0)),
        out_shape=jax.ShapeDtypeStruct(shape, f32),
        input_output_aliases=aliases,
        compiler_params=ROOM,
        cost_estimate=pl.CostEstimate(flops=0, bytes_accessed=6 * count * size * LANES, transcendentals=0),
    )(spot, *arrays, spot if total is None else total)


def split(value):
    high = value.astype(bf16)
    return high, (value - high.astype(f32)).astype(bf16)


def dot(a, b):
    return jnp.dot(a, b, preferred_element_type=f32)


def dot_right(value, matrix, at):
    high, low = split(value)
    return dot(high, matrix[at]) + (dot(low, matrix[at]) + dot(high, matrix[at + 1]))


def dot_left(matrix, at, value):
    high, low = split(value)
    return dot(matrix[at], high) + (dot(matrix[at], low) + dot(matrix[at + 1], high))


def times_right(x, matrix, ready=(), finish=None):
    for copy in ready[:1]:
        copy.wait()
    k1 = dot_right(x[0] + x[1], matrix, 0)
    for copy in ready[1:2]:
        copy.wait()
    k3 = dot_right(x[1], matrix, 4)
    real = k1 - k3
    if finish is not None:
        finish(0, real)
    for copy in ready[2:]:
        copy.wait()
    k2 = dot_right(x[0], matrix, 2)
    if finish is not None:
        finish(1, k1 + k2)
    return real, k1 + k2


def times_left(matrix, x):
    k1 = dot_left(matrix, 0, x[0] + x[1])
    k2 = dot_left(matrix, 2, x[0])
    k3 = dot_left(matrix, 4, x[1])
    return k1 - k3, k1 + k2


class Copies:
    def __init__(self, sems):
        self.sems = sems
        self.count = 0

    def start(self, source, target):
        copy = pltpu.make_async_copy(source, target, self.sems.at[self.count])
        self.count += 1
        copy.start()
        return copy


def precondition(x_scr, given, held, copies, fill, finish, last=None):
    u_ref, ut_ref, factor_ref = held[:3]
    ready = [copies.start(given[0].at[pl.ds(at, 2)], u_ref.at[pl.ds(at, 2)]) for at in (0, 4, 2)]
    copy = copies.start(given[1], ut_ref)
    scaling = copies.start(given[2], factor_ref)
    fill()
    y = times_right((x_scr[0], x_scr[1]), u_ref, ready)
    copy.wait()
    y = times_left(ut_ref, y)
    scaling.wait()
    if last is not None:
        last()
    y = complex_product(y, (factor_ref[0], factor_ref[1]))
    y = times_left(u_ref, y)
    times_right(y, ut_ref, (), finish)


def p_scratch(points, count, pieces):
    matrix = pltpu.VMEM((6, points, points), bf16)
    field = pltpu.VMEM((2, points, points), f32)
    return [field, matrix, matrix] + [field] * (count - 2) + [pltpu.SemaphoreType.DMA((pieces + 8,))]


def prepare_kernel(shift_energy_ref, shift_width_ref, vec_ref, energy_ref, width_ref, u_ref, ut_ref, factor_ref):
    real, imag = vec_ref[0], vec_ref[1]
    for out, (r, i) in ((u_ref, (real, imag)), (ut_ref, (real.T, imag.T))):
        for at, value in enumerate((r, i - r, r + i)):
            high, low = split(value)
            out[2 * at] = high
            out[2 * at + 1] = low
    points = real.shape[0]

    def both(ref):
        column = jnp.broadcast_to(ref[...], (LANES, points)).T
        return jnp.concatenate([column] * (points // LANES), axis=1) + ref[...]

    den_real = both(energy_ref) - shift_energy_ref[0]
    den_imag = -both(width_ref) - shift_width_ref[0]
    modulus = den_real * den_real + den_imag * den_imag
    factor_ref[0] = den_real / modulus
    factor_ref[1] = -den_imag / modulus


def prepare(eigenvectors, energies, widths, shift_energy, shift_width):
    points = eigenvectors.shape[1]
    matrix = jax.ShapeDtypeStruct((6, points, points), bf16)
    return pl.pallas_call(
        prepare_kernel,
        in_specs=[SMEM] * 2 + [VMEM] * 3,
        out_specs=[VMEM] * 3,
        out_shape=[matrix, matrix, jax.ShapeDtypeStruct((2, points, points), f32)],
        compiler_params=ROOM,
        cost_estimate=pl.CostEstimate(flops=0, bytes_accessed=24 * points * points, transcendentals=0),
    )(shift_energy, shift_width, eigenvectors, energies[None, :], widths[None, :])


def p_cost(points):
    return pl.CostEstimate(flops=36 * 2 * points**3, bytes_accessed=16 * points * points, transcendentals=0)


def fill_from_rows(pieces, refs, x_scr, me, rows, points):
    for d, piece in enumerate(refs):
        base = pieces.place(d, me) * rows
        if not pieces.natural:
            base = pl.multiple_of(base, rows)

        def put(q, row, column, value):
            x_scr[q, pl.ds(base + row, GROUP_ROWS), pl.ds(column, LANES)] = value

        decode_piece(lambda row: piece[pl.ds(row, GROUP_ROWS), :], rows, points, put)


def first_kernel(plan, shared, pieces, spot_ref, *refs):
    rad, chan, rows, points, column_cuts, height = plan
    given, first_ref, outs = refs[rad : rad + 3], refs[rad + 3], refs[rad + 4 : -6]
    in_scr, x_scr, held, sems = refs[-6], refs[-5], refs[-4:-1], refs[-1]
    me, z_me = spot_ref[0], spot_ref[1]
    copies = Copies(sems)
    views = pieces.views(refs[:rad], piece_rows(rows, points))
    arriving = [copies.start(view, in_scr.at[p]) for p, view in enumerate(views)]
    leaving = []

    def fill():
        for copy in arriving:
            copy.wait()
        fill_from_rows(pieces, [in_scr.at[p] for p in range(rad)], x_scr, me, rows, points)

    def finish(q, value):
        x_scr[q] = value
        leaving.append(copies.start(x_scr.at[q], first_ref.at[q]))
        if shared is None:
            rounded = value.astype(bf16)
            for z in range(chan):
                column = (z % column_cuts) * LANES
                for p in range(rad):
                    row = p * rows + (z // column_cuts) * height
                    outs[0][z * rad + p, q] = rounded[row : row + height, column : column + LANES]
        else:
            for d in range(shared):
                row = pl.multiple_of((me ^ d) * rows, rows)
                for e in range(chan):
                    column = pl.multiple_of((z_me ^ e) * LANES, LANES)
                    outs[d][e, q] = x_scr[q, pl.ds(row, height), pl.ds(column, LANES)].astype(bf16)

    precondition(x_scr, given, held, copies, fill, finish)
    for copy in leaving:
        copy.wait()


def first_round(pieces, u, ut, factor, spot, plan, shared=None):
    rad, chan, rows, points, column_cuts, height = plan
    size = piece_rows(rows, points)
    if shared is None:
        sent = [jax.ShapeDtypeStruct((chan * rad, 2, height, LANES), bf16)]
    else:
        sent = [jax.ShapeDtypeStruct((chan, 2, height, LANES), bf16)] * shared
    result = pl.pallas_call(
        functools.partial(first_kernel, plan, shared, pieces),
        in_specs=[SMEM] + [ANY] * (rad + 3),
        out_specs=[ANY] + [VMEM] * len(sent),
        out_shape=[jax.ShapeDtypeStruct((2, points, points), f32)] + sent,
        scratch_shapes=[pltpu.VMEM((rad, size, LANES), i16)] + p_scratch(points, 3, rad),
        compiler_params=ROOM,
        cost_estimate=p_cost(points),
    )(spot, *pieces.arrays(), u, ut, factor)
    return result[0], result[1:]


def second_kernel(plan, shared, natural, pieces, spot_ref, *refs):
    rad, chan, rows, points, column_cuts, height = plan
    taken = 1 if shared is None else rad
    given, outs = refs[taken : taken + 4], refs[taken + 4 : -9]
    in_scr, code_scr, exp_scr, x_scr = refs[-9:-5]
    held, sems = refs[-5:-1], refs[-1]
    me, z_me = spot_ref[0], spot_ref[1]
    copies = Copies(sems)
    if shared is None:
        arriving = [copies.start(refs[0], in_scr)]
    else:
        views = pieces.views(refs[:rad], chan)
        arriving = [copies.start(view, in_scr.at[pl.ds(d * chan, chan)]) for d, view in enumerate(views)]
    groups = rows // GROUP_ROWS
    kept = []

    def fill():
        for copy in arriving:
            copy.wait()
        for q in range(2):
            if shared is None:
                for z in range(chan):
                    column = (z % column_cuts) * LANES
                    for p in range(rad):
                        row = p * rows + (z // column_cuts) * height
                        x_scr[q, pl.ds(row, height), pl.ds(column, LANES)] = in_scr[z * rad + p, q].astype(f32)
            else:
                for d in range(rad):
                    row = pl.multiple_of((me ^ d) * rows, rows)
                    for e in range(chan):
                        column = pl.multiple_of((z_me ^ e) * LANES, LANES)
                        x_scr[q, pl.ds(row, height), pl.ds(column, LANES)] = in_scr[d * chan + e, q].astype(f32)

    def last():
        kept.append(copies.start(given[3], held[3]))

    def finish(q, value):
        if q == 0:
            kept[0].wait()
        codes, exponents = coded_parts([held[3][q] - value])
        for c, code in enumerate(codes[0]):
            code_scr[q, c] = code
        for p in range(rad):
            exp_scr[p, pl.ds(q * groups, groups), :] = exponents[0][p * groups : (p + 1) * groups]

    precondition(x_scr, given, held, copies, fill, finish, last)
    chunks = points // LANES
    size = piece_rows(rows, points)
    for d in range(rad if shared is None else shared):
        spot = d if natural else me ^ d
        row = d * rows if natural else pl.multiple_of(spot * rows, rows)
        if natural:
            out_ref, base = outs[0], d * size
        elif shared is None:
            out_ref, base = outs[d // 2], (d % 2) * size
        else:
            out_ref, base = outs[d], 0
        for q in range(2):
            for c in range(chunks):
                out_ref[pl.ds(base + (q * chunks + c) * rows, rows), :] = code_scr[q, c, pl.ds(row, rows), :]
        out_ref[pl.ds(base + 2 * chunks * rows, GROUP_ROWS), :] = tail_of([exp_scr[spot]])


def tail_rows(rows):
    return 2 * (rows // GROUP_ROWS)


def second_round(pieces, first, u, ut, factor, spot, plan, shared=None, natural=False):
    rad, chan, rows, points, column_cuts, height = plan
    size = piece_rows(rows, points)
    if natural:
        shapes = [jax.ShapeDtypeStruct((rad * size, LANES), i16)]
    elif shared is None:
        shapes = [jax.ShapeDtypeStruct((2 * size, LANES), i16)] * (rad // 2)
    else:
        shapes = [jax.ShapeDtypeStruct((size, LANES), i16)] * shared
    given = [pieces] if shared is None else pieces.arrays()
    return pl.pallas_call(
        functools.partial(second_kernel, plan, shared, natural, pieces),
        in_specs=[SMEM] + [ANY] * (len(given) + 4),
        out_specs=[VMEM] * len(shapes),
        out_shape=shapes,
        scratch_shapes=[
            pltpu.VMEM((chan * rad, 2, height, LANES), bf16),
            pltpu.VMEM((2, points // LANES, points, LANES), i16),
            pltpu.VMEM((rad, tail_rows(rows), LANES), f32),
        ]
        + p_scratch(points, 4, len(given)),
        compiler_params=ROOM,
        cost_estimate=p_cost(points),
    )(spot, *given, u, ut, factor, first)


def weights_kernel(layout, channel_ref, partners_ref, multipole_ref, counts_ref, angular_ref, out_ref):
    chan, rad, full, live = layout
    links, channels = partners_ref.shape
    slots = out_ref.shape[1]
    group = channels // chan
    exact = dict(precision=lax.Precision.HIGHEST, preferred_element_type=f32)
    last = (((1,), (1,)), ((), ()))

    def ids(shape, axis):
        return lax.broadcasted_iota(i32, shape, axis)

    at, slot = ids((slots, channels), 0), ids((slots, channels), 1)
    z, inner = slot // group, slot % group
    found = (inner // rad) * (chan * rad) + z * rad + inner % rad
    if live:
        found = jnp.where(inner < full * rad, found, full * chan * rad + z * live + inner - full * rad)
    place = (at == found).astype(f32)
    held = (channel_ref[...] == ids((channels, channels), 0)).astype(f32)
    hot = lax.dot_general(place, held, last, **exact)
    tables = [jnp.zeros((channels, channels), f32) for _ in range(ORDERS)]
    for link in range(links):
        row = slice(link, link + 1)
        weight = jnp.where(counts_ref[...] > link, angular_ref[row, :], 0.0)
        spread = jnp.where(partners_ref[row, :] == ids((channels, channels), 0), weight, 0.0)
        for k in range(ORDERS):
            tables[k] = tables[k] + jnp.where(multipole_ref[row, :] == k, spread, 0.0)
    for k in range(ORDERS):
        targets = lax.dot_general(hot, tables[k], last, **exact)
        coupling = lax.dot_general(targets, hot, last, **exact)
        high, low = split(coupling)
        out_ref[k, :, 0:slots] = high
        out_ref[k, :, slots : 2 * slots] = low


def coupling_weights(slot_channel, partners, multipole, counts, angular, layout):
    chan, rad, full, live = layout
    slots = (full + (live > 0)) * chan * rad
    return pl.pallas_call(
        functools.partial(weights_kernel, layout),
        in_specs=[VMEM] * 5,
        out_specs=VMEM,
        out_shape=jax.ShapeDtypeStruct((ORDERS, slots, 2 * slots), bf16),
        compiler_params=ROOM,
        cost_estimate=pl.CostEstimate(flops=0, bytes_accessed=8 << 20, transcendentals=0),
    )(slot_channel[None, :], partners.T, multipole.T, counts[None, :], angular.T)


PACK = 4


def gather_kernel(shared, spot_ref, *refs):
    out_ref, scr = refs[-2], refs[-1]
    per = out_ref.shape[2]
    height = scr.shape[0] // per
    for q in range(2):
        if shared is None:
            for d in range(per):
                scr[pl.ds(d * height, height), :] = refs[0][d, q].astype(f32)
        else:
            scr[...] = jnp.zeros_like(scr)
            for e, ref in enumerate(refs[:-2]):
                for d in range(shared):
                    at = (spot_ref[1] ^ e) * shared + ((spot_ref[0] ^ d) & (shared - 1))
                    scr[pl.ds(pl.multiple_of(at * height, height), height), :] = ref[d, q].astype(f32)
        for r in range(height):
            value = scr[pl.ds(r, per, stride=height), :]
            out_ref[q, r // PACK, :, pl.ds((r % PACK) * LANES, LANES)] = value.astype(bf16)


def gather_round(pieces, spot, per, shared=None):
    height = pieces[0].shape[2]
    return pl.pallas_call(
        functools.partial(gather_kernel, shared),
        in_specs=[SMEM] + [VMEM] * len(pieces),
        out_specs=VMEM,
        out_shape=jax.ShapeDtypeStruct((2, height // PACK, per, PACK * LANES), bf16),
        scratch_shapes=[pltpu.VMEM((per * height, LANES), f32)],
        compiler_params=LEAN,
        cost_estimate=pl.CostEstimate(flops=0, bytes_accessed=8 * per * height * LANES, transcendentals=0),
    )(spot, *pieces)


def couple_kernel(sources, at, per, shared, spot_ref, weight_ref, table_ref, *refs):
    xs, scr = refs[:sources], refs[-1]
    outs = refs[sources:-1]
    packs = xs[0].shape[1]
    height = packs * PACK
    weight = weight_ref[:, at : at + per, :].reshape(ORDERS * per, weight_ref.shape[2])

    def step(g, carry):
        mixed = []
        for q in range(2):
            values = [x[q, g] for x in xs]
            mixed.append(dot(weight, jnp.concatenate(values + values, axis=0)))
        inverse = (table_ref[0, pl.ds(g, 1), :], table_ref[1, pl.ds(g, 1), :])
        ratio = (table_ref[2, pl.ds(g, 1), :], table_ref[3, pl.ds(g, 1), :])
        total = [mixed[q][(ORDERS - 1) * per :] for q in range(2)]
        for k in range(ORDERS - 2, -1, -1):
            total = complex_product(total, ratio)
            total = [total[q] + mixed[q][k * per : (k + 1) * per] for q in range(2)]
        total = complex_product(total, inverse)
        for q in range(2):
            for r in range(PACK):
                scr[q, pl.ds(g * PACK + r, per, stride=height), :] = total[q][:, r * LANES : (r + 1) * LANES]
        return carry

    lax.fori_loop(0, packs, step, 0, unroll=2)
    for q in range(2):
        if shared is None:
            for d in range(per):
                outs[0][d, q] = scr[q, pl.ds(d * height, height), :].astype(bf16)
        else:
            for e, out_ref in enumerate(outs):
                for d in range(shared):
                    slot = (spot_ref[1] ^ e) * shared + ((spot_ref[0] ^ d) & (shared - 1))
                    row = pl.multiple_of(slot * height, height)
                    out_ref[d, q] = scr[q, pl.ds(row, height), :].astype(bf16)


def couple_round(gathered, weights, table, spot, at, chan, per, shared=None):
    _, packs, _, width = gathered[0].shape
    height = packs * PACK
    slots = weights.shape[2]
    if shared is None:
        outs = [jax.ShapeDtypeStruct((per, 2, height, LANES), bf16)]
    else:
        outs = [jax.ShapeDtypeStruct((shared, 2, height, LANES), bf16)] * chan
    return pl.pallas_call(
        functools.partial(couple_kernel, len(gathered), at, per, shared),
        in_specs=[SMEM] + [VMEM] * (2 + len(gathered)),
        out_specs=[VMEM] * len(outs),
        out_shape=outs,
        scratch_shapes=[pltpu.VMEM((2, per * height, LANES), f32)],
        compiler_params=LEAN,
        cost_estimate=pl.CostEstimate(
            flops=32 * packs * per * slots * width, bytes_accessed=6 << 20, transcendentals=0
        ),
    )(spot, weights, table, *gathered)


def kernel_table(row_ids, col_ids, points):
    upper = contour(jnp.maximum(row_ids[:, None], col_ids[None, :]), points)
    lower = contour(jnp.minimum(row_ids[:, None], col_ids[None, :]), points)
    modulus = upper[0] * upper[0] + upper[1] * upper[1]
    inverse = (upper[0] / modulus, -upper[1] / modulus)
    ratio = complex_product(lower, inverse)
    return jnp.stack([inverse[0], inverse[1], ratio[0], ratio[1]])


def local(
    vectors,
    eigenvectors,
    energies,
    widths,
    shift_energy,
    shift_width,
    slot_channel,
    partners,
    multipole,
    counts,
    angular,
):
    _, _, group, rows, points = vectors.shape
    chan = lax.axis_size("chan")
    rad = lax.axis_size("rad")
    column_cuts = min(chan, points // LANES)
    height = rows // (chan // column_cuts)
    plan = (rad, chan, rows, points, column_cuts, height)
    full, live = group // rad, group % rad
    if live != 2 or column_cuts != chan:
        full, live = full + 1, 0
    spot = jnp.stack([lax.axis_index("rad"), lax.axis_index("chan")]).astype(i32)

    def over(piece, axis, size, d):
        return lax.ppermute(piece, axis, [(i, i ^ d) for i in range(size)])

    def over_even(arrays):
        return [arrays[0]] + [over(array, "rad", rad, 2 * e) for e, array in enumerate(arrays) if e]

    def over_next(got, count, halves=None):
        swapped = over(second_halves(got) if halves is None else halves, "rad", rad, 1)
        return [
            Pieces([(swapped, (d // 2) * count + j) if d % 2 else (got[d // 2], j) for d in range(rad)], False)
            for j in range(count)
        ]

    def over_chan(pieces):
        return [pieces[0]] + [over(piece, "chan", chan, e) for e, piece in enumerate(pieces) if e]

    def over_all(piece):
        return lax.all_to_all(piece, ("chan", "rad"), 0, 0, tiled=True)

    def share(piece):
        flat = lax.all_to_all(piece.reshape(rad, -1, LANES), "rad", 0, 0, tiled=True).reshape(-1, LANES)
        return Pieces([(flat, p) for p in range(rad)], True)

    rounds = [(j * rad, min(rad, group - j * rad)) for j in range(full)]
    if live:
        rounds.append((full * rad, live))
    everyone = chan * rad

    def cut(values):
        is_pieces = lambda v: isinstance(v, Pieces)
        leaves, tree = jax.tree.flatten(values, is_leaf=is_pieces)
        arrays = {}
        for leaf in leaves:
            for array in leaf.arrays() if is_pieces(leaf) else [leaf]:
                arrays[id(array)] = array
        tied = dict(zip(arrays, lax.optimization_barrier(list(arrays.values()))))
        leaves = [
            Pieces([(tied[id(array)], at) for array, at in leaf.blocks], leaf.natural)
            if is_pieces(leaf)
            else tied[id(leaf)]
            for leaf in leaves
        ]
        return jax.tree.unflatten(tree, leaves)

    near = [encode_rounds(vectors, [r], rad, spot, True)[0] for r in rounds[:2]]
    far = [encode_rounds(vectors, [r], rad, spot, False) for r in rounds[2:3]]
    u, ut, factor = prepare(eigenvectors, energies, widths, shift_energy, shift_width)
    small = (slot_channel, partners, multipole, counts, angular, spot)
    received, near, far, u, ut, factor, small, later = cut((share(near[0]), near, far, u, ut, factor, small, vectors))

    def apply_first(pieces, shared=None):
        return first_round(pieces, u, ut, factor, spot, plan, shared)

    def constants(small):
        weights = coupling_weights(*small[:5], (chan, rad, full, live))
        z = small[5][1]
        row_ids = small[5][0] * rows + (z // column_cuts) * height + jnp.arange(height, dtype=i32)
        col_ids = (z % column_cuts) * LANES + jnp.arange(LANES, dtype=i32)
        return weights, kernel_table(row_ids, col_ids, points).reshape(4, height // PACK, PACK * LANES)

    firsts, gathered, arriving, fixed, halves = [], [], (), None, None
    first, pieces = apply_first(received)
    firsts.append(first)
    if len(near) > 1:
        received = share(near[1])
    flying, received, small, far, later = cut((pieces[0], received, small, far, later))
    for j in range(1, len(rounds)):
        flying = over_all(flying)
        if j > 1:
            received = over_next(arriving, 1, halves)[0]
        arriving = over_even(far[j - 1]) if j - 1 < len(far) else ()
        if j == 1:
            far += [encode_rounds(later, [r], rad, spot, False) for r in rounds[3:]]
        if j == full:
            fixed = constants(small)
        first, pieces = apply_first(received, live if j == full else None)
        firsts.append(first)
        if j == full:
            pieces = [pieces[0]] + [over(piece, "rad", rad, d) for d, piece in enumerate(pieces) if d]
            pieces = over_chan([jnp.stack([piece[e] for piece in pieces]) for e in range(chan)])
        halves = second_halves(arriving) if arriving and j > 1 else None
        flown, pieces, small, far, arriving, gathered, fixed, halves = cut(
            (flying, pieces, small, far, arriving, gathered, fixed, halves)
        )
        flying = pieces[0]
        gathered.append(gather_round([flown], spot, everyone))
    if not live:
        gathered.append(gather_round([over_all(flying)], spot, everyone))
    weights, table = fixed or constants(small)
    if live:
        gathered.append(gather_round(pieces, spot, everyone, live))

    def couple(j):
        if j == full:
            return couple_round(gathered, weights, table, spot, full * everyone, chan, chan * live, live)
        return couple_round(gathered, weights, table, spot, j * everyone, chan, everyone)[0]

    def apply_second(pieces, j, shared=None):
        return second_round(pieces, firsts[j], u, ut, factor, spot, plan, shared, shared is None and j >= full - 2)

    coupled, gathered, firsts = cut((couple(0), gathered, firsts))
    coupled = [coupled]
    update, shared, total, ready = None, None, None, []
    for j in range(full):
        flown = over_all(coupled[j])
        if j == 0:
            coupled += [couple(k) for k in range(1, full)]
            shared = over_chan(couple(full)) if live else None
        if live and j == min(1, full - 1):
            both = jnp.concatenate([jnp.stack([piece[d] for piece in shared]) for d in range(live)])
            shared = over_even([both] * (rad // 2))
        elif live and j == min(2, full - 1):
            shared = over_next(shared, 1)[0]
        if j > 2:
            ready[j - 3] = over_next(ready[j - 3], 1)[0]
        if update is not None:
            ready.append(over_even(update) if len(update) > 1 else update)
        update = apply_second(mine, j - 1) if j > 0 else None
        mine, coupled, update, ready, shared = cut((flown, coupled, update, ready, shared))
    ready = [over_next(got, 1)[0] if isinstance(got, list) else got for got in ready]
    if live and full < 3:
        shared = over_next(shared, 1)[0]
    if update is not None:
        ready.append(share(update[0]))
    update = apply_second(mine, full - 1)
    update, ready, shared = cut((update, ready, shared))
    done = share(update[0])
    if ready:
        total = decode_rounds(ready, total, rounds[: len(ready)], spot, vectors.shape)
    if live:
        extra = apply_second(shared, full, live)
        done, extra, total = cut((done, extra, total))
        extra = [extra[0]] + [over(piece, "rad", rad, d) for d, piece in enumerate(extra) if d]
        extra = Pieces([(piece, 0) for piece in extra], False)
    total = decode_rounds([done], total, rounds[full - 1 : full], spot, vectors.shape)
    if live:
        total = decode_rounds([extra], total, rounds[full:], spot, vectors.shape)
    return total


def solution(mesh):
    in_specs = (P(None, None, "chan", "rad", None),) + (P(),) * 10
    out_specs = P(None, None, "chan", "rad", None)
    return jax.shard_map(local, mesh=mesh, in_specs=in_specs, out_specs=out_specs, check_vma=False)
```
